32 devices in a mesh: lon: 8 (over y, x, core), lat: 4 (over z).
Axes of the slice: x: 2, y: 2, z: 4, core: 2. Of those that a mesh axis runs over, the one named last changes fastest.
Arguments:
- temp: float32 [4, 256, 6144], P(None, 'lat', 'lon'), may hold values from -6 to 6
- salt: float32 [4, 256, 6144], P(None, 'lat', 'lon'), may hold values from -6 to 6
- uvel: float32 [4, 256, 6144], P(None, 'lat', 'lon'), may hold values from -6 to 6
- vvel: float32 [4, 256, 6144], P(None, 'lat', 'lon'), may hold values from -6 to 6
- thick: float32 [4, 256, 6144], P(None, 'lat', 'lon'), may hold values from 0.5 to 2
- land: int32 [4, 256, 6144], P(None, 'lat', 'lon'), may hold values 0 or 1
- east_width: float32 [256, 6144], P('lat', 'lon'), may hold values from 0.5 to 2
- north_width: float32 [256, 6144], P('lat', 'lon'), may hold values from 0.5 to 2
- coriolis: float32 [256, 6144], P('lat', 'lon'), may hold values from 0.5 to 1.5
Outputs:
- temp_next: float32 [4, 256, 6144], P(None, 'lat', 'lon')
- salt_next: float32 [4, 256, 6144], P(None, 'lat', 'lon')
- uvel_next: float32 [4, 256, 6144], P(None, 'lat', 'lon')
- vvel_next: float32 [4, 256, 6144], P(None, 'lat', 'lon')
The draws below stay inside these ranges and needn't reach their ends.
All inputs are finite; a program needn't handle non-finite values. No bound on the sum of `land` on one device may be relied on, other than what follows from the above.
Results may differ from the reference program's by a relative error of at most 0.00002.
Values sent between devices are 32-bit elements; how exact they have to be, the bound alone decides.
A program may use at most 128 MiB of HBM per device.

```python
import math
import jax
import jax.numpy as jnp

LEV = 4
NLAT = 256
NLON = 6144


def place_ends(values, own_key, smallest, largest):
    place = [jax.random.randint(jax.random.fold_in(own_key, axis), (), 0, length) for axis, length in enumerate(values.shape)]
    main_axis = values.shape.index(max(values.shape))
    beside = place[:main_axis] + [(place[main_axis] + 1) % values.shape[main_axis]] + place[main_axis + 1:]
    return values.at[tuple(place)].set(smallest).at[tuple(beside)].set(largest)


def block_levels(own_key, dims, pieces, smallest, top_value):
    def one(axis_at, blocks):
        heights = jax.random.uniform(jax.random.fold_in(jax.random.fold_in(own_key, 6), axis_at), (blocks,), jnp.float32, smallest / len(pieces), top_value / len(pieces))
        return jnp.repeat(jnp.exp(heights), dims[axis_at] // blocks).reshape((-1,) + (1,) * (len(dims) - axis_at - 1))

    gain = one(*pieces[0])
    for cut in pieces[1:]:
        gain = gain * one(*cut)
    return gain


def scatter_about(rng, dims, spread, bound, split=(), dtype=jnp.bfloat16):
    drawn = spread * jax.random.normal(rng, dims, jnp.float32)
    if split:
        drawn = drawn * block_levels(rng, dims, split, -0.22, 0.18)
    return jnp.clip(drawn, -bound, bound).astype(dtype)


def setup_inputs(seed: int = 0) -> dict:
    key_of = jax.random.split(jax.random.key(seed), 10)
    return {
        "temp": scatter_about(key_of[0], (LEV, NLAT, NLON), 1.0, 6.0, ((1, 4), (2, 8)), jnp.float32),
        "salt": scatter_about(key_of[1], (LEV, NLAT, NLON), 1.0, 6.0, ((1, 4), (2, 8)), jnp.float32),
        "uvel": scatter_about(key_of[2], (LEV, NLAT, NLON), 1.0, 6.0, ((1, 4), (2, 8)), jnp.float32),
        "vvel": scatter_about(key_of[3], (LEV, NLAT, NLON), 1.0, 6.0, ((1, 4), (2, 8)), jnp.float32),
        "thick": jnp.clip(jnp.exp(math.log(2.0) - 1.3862944 * jax.random.uniform(key_of[4], (LEV, NLAT, NLON), jnp.float32) ** block_levels(key_of[4], (LEV, NLAT, NLON), ((1, 4), (2, 8)), -0.2, 0.2)), 0.5, 2.0),
        "land": place_ends((jax.random.randint(key_of[5], (LEV, NLAT, NLON), 0, 4) < 3).astype(jnp.int32), jax.random.fold_in(key_of[5], 1), 0, 1),
        "east_width": jnp.clip(jnp.exp(math.log(2.0) - 1.3862944 * jax.random.uniform(key_of[6], (NLAT, NLON), jnp.float32) ** block_levels(key_of[6], (NLAT, NLON), ((0, 4), (1, 8)), -0.2, 0.2)), 0.5, 2.0),
        "north_width": jnp.clip(jnp.exp(math.log(2.0) - 1.3862944 * jax.random.uniform(key_of[7], (NLAT, NLON), jnp.float32) ** block_levels(key_of[7], (NLAT, NLON), ((0, 4), (1, 8)), -0.2, 0.2)), 0.5, 2.0),
        "coriolis": jnp.clip(0.5 + 1.0 * jax.random.uniform(key_of[8], (NLAT, NLON), jnp.float32) ** block_levels(key_of[8], (NLAT, NLON), ((0, 4), (1, 8)), -0.2, 0.2), 0.5, 1.5),
    }


time_step = 0.2
biharm_coef = 0.02
alpha_temp = 0.2
beta_salt = 0.8
thin_floor = 0.25


def laplace(field, east_coef, north_coef, volume):
    east_diff = east_coef * (field[..., 1:] - field[..., :-1])
    north_diff = north_coef * (field[..., 1:, :] - field[..., :-1, :])
    return (east_diff[..., 1:-1, 1:] - east_diff[..., 1:-1, :-1] + north_diff[..., 1:, 1:-1] - north_diff[..., :-1, 1:-1]) / volume


def advance_level(fields, depth_ext, east_ext, north_ext, overhead, wet_cells, coriolis, east_width, north_width):
    lon_thick = jnp.minimum(depth_ext[:, :-1], depth_ext[:, 1:])
    lat_thick = jnp.minimum(depth_ext[:-1], depth_ext[1:])
    east_coef = lon_thick * (north_ext[:, :-1] + north_ext[:, 1:]) / (east_ext[:, :-1] + east_ext[:, 1:])
    north_coef = lat_thick * (east_ext[:-1] + east_ext[1:]) / (north_ext[:-1] + north_ext[1:])
    volume = east_ext * north_ext * jnp.maximum(depth_ext, thin_floor)
    cycle_lap = laplace(fields, east_coef, north_coef, volume[1:-1, 1:-1])
    biharmonic = laplace(cycle_lap, east_coef[1:-1, 1:-1], north_coef[1:-1, 1:-1], volume[2:-2, 2:-2])
    transport_east = lon_thick * (north_ext[:, :-1] + north_ext[:, 1:]) * (fields[2][:, :-1] + fields[2][:, 1:]) / 4.0
    transport_north = lat_thick * (east_ext[:-1] + east_ext[1:]) * (fields[3][:-1] + fields[3][1:]) / 4.0
    tracers = fields[:2]
    flux_east = transport_east * (tracers[..., :-1] + tracers[..., 1:]) / 2.0
    flux_north = transport_north * (tracers[..., :-1, :] + tracers[..., 1:, :]) / 2.0
    advect = (flux_east[..., 2:-2, 2:-1] - flux_east[..., 2:-2, 1:-2] + flux_north[..., 2:-1, 2:-2] - flux_north[..., 1:-2, 2:-2]) / volume[2:-2, 2:-2]
    buoyancy = (beta_salt * fields[1] - alpha_temp * fields[0]) * depth_ext
    pressure = overhead + 0.5 * buoyancy
    overhead = overhead + buoyancy
    grad_east = (pressure[2:-2, 3:-1] - pressure[2:-2, 1:-3]) / (2.0 * east_width)
    grad_north = (pressure[3:-1, 2:-2] - pressure[1:-3, 2:-2]) / (2.0 * north_width)
    interior = fields[:, 2:-2, 2:-2]
    temp_out = wet_cells * (interior[0] - time_step * advect[0] - biharm_coef * biharmonic[0])
    salt_out = wet_cells * (interior[1] - time_step * advect[1] - biharm_coef * biharmonic[1])
    uvel_out = wet_cells * (interior[2] + time_step * (coriolis * interior[3] - grad_east) - biharm_coef * biharmonic[2])
    vvel_out = wet_cells * (interior[3] + time_step * (-coriolis * interior[2] - grad_north) - biharm_coef * biharmonic[3])
    return (temp_out, salt_out, uvel_out, vvel_out), overhead


def extend_global(stacked, sign_list):
    mirror = stacked[:, -3:, ::-1] * sign_list[:, None, None]
    ghost_rows = jnp.stack([mirror[:, 1], mirror[:, 0]], axis=1)
    rim_fill = jnp.array([0.0, 0.0, 0.0, 0.0, 0.0, 1.0, 1.0], jnp.float32)
    south_rim = jnp.zeros((stacked.shape[0], 2, stacked.shape[2]), jnp.float32) + rim_fill[:, None, None]
    tall_stack = jnp.concatenate([south_rim, stacked, ghost_rows], axis=1)
    return jnp.concatenate([tall_stack[..., -2:], tall_stack, tall_stack[..., :2]], axis=2)


def reference(temp, salt, uvel, vvel, thick, land, east_width, north_width, coriolis):
    depth = land.astype(jnp.float32) * thick
    sign_list = jnp.array([1.0, 1.0, -1.0, -1.0, 1.0, 1.0, 1.0], jnp.float32)
    overhead = jnp.zeros((temp.shape[1] + 4, temp.shape[2] + 4), jnp.float32)
    results = []
    for level_index in range(temp.shape[0]):
        stacked = jnp.stack([temp[level_index], salt[level_index], uvel[level_index], vvel[level_index], depth[level_index], east_width, north_width])
        extended = extend_global(stacked, sign_list)
        outputs, overhead = advance_level(extended[:4], extended[4], extended[5], extended[6], overhead, land[level_index].astype(jnp.float32), coriolis, east_width, north_width)
        results.append(outputs)
    return (jnp.stack([r[0] for r in results]), jnp.stack([r[1] for r in results]), jnp.stack([r[2] for r in results]), jnp.stack([r[3] for r in results]))
```

```python
import functools

import jax
import jax.numpy as jnp
from jax import lax
from jax.experimental import pallas as pl
from jax.experimental.pallas import tpu as pltpu
from jax.sharding import PartitionSpec as P

time_step = 0.2
biharm_coef = 0.02
alpha_temp = 0.2
beta_salt = 0.8
thin_floor = 0.25

LANES = 128
PAD = 8


def kernel(
    n_lat, n_lon,
    temp, salt, uvel, vvel, thick, land, east_width, north_width, coriolis,
    temp_out, salt_out, uvel_out, vvel_out,
    q, th, la, cor, lap, cf, pres, base, ob,
    row_pack, row_recv, col_pack, corner_pack, col_recv,
    in_sem, out_sem, row_send, row_sem, col_send, col_sem, corner_send,
):
    levels, rows, width = temp.shape
    nc = width // LANES
    nb = rows // 8
    nf = 5 * levels + 2
    fa, fb = 5 * levels, 5 * levels + 1
    lat, lon = lax.axis_index("lat"), lax.axis_index("lon")
    top = lat == n_lat - 1
    south = lat > 0
    east_lon = lax.rem(lon + 1, n_lon)
    west_lon = lax.rem(lon + n_lon - 1, n_lon)
    lat_n = jnp.where(top, lat, lat + 1)
    lat_s = jnp.where(south, lat - 1, 0)
    north = (lat_n, jnp.where(top, n_lon - 1 - lon, lon))
    fold_e = lax.rem(2 * n_lon - 2 - lon, n_lon)
    fold_w = lax.rem(n_lon - lon, n_lon)
    north_e = (lat_n, jnp.where(top, fold_e, east_lon))
    north_w = (lat_n, jnp.where(top, fold_w, west_lon))
    e_self = jnp.logical_and(top, fold_e == lon)
    w_self = jnp.logical_and(top, fold_w == lon)
    e_far, w_far = jnp.logical_not(e_self), jnp.logical_not(w_self)
    east, west = (lat, east_lon), (lat, west_lon)

    barrier = pltpu.get_barrier_semaphore()

    def greet(where):
        pl.semaphore_signal(barrier, inc=1, device_id={"lat": where[0], "lon": where[1]}, device_id_type=pl.DeviceIdType.MESH)

    greet(east)
    greet(west)
    greet(north)

    @pl.when(e_far)
    def _():
        greet(north_e)

    @pl.when(w_far)
    def _():
        greet(north_w)

    @pl.when(south)
    def _():
        greet((lat_s, lon))
        greet((lat_s, east_lon))
        greet((lat_s, west_lon))

    order = [0, nc - 1] + list(range(1, nc - 1))
    loads = {}
    sem_at = 0
    for c in order:
        cols = pl.ds(c * LANES, LANES)
        here = []
        for src, dst in (
            (land, la.at[:, c]),
            (thick, th.at[:, c]),
            (temp, q.at[0:levels, c, PAD:PAD + rows]),
            (salt, q.at[levels:2 * levels, c, PAD:PAD + rows]),
            (uvel, q.at[2 * levels:3 * levels, c, PAD:PAD + rows]),
            (vvel, q.at[3 * levels:4 * levels, c, PAD:PAD + rows]),
        ):
            here.append(pltpu.make_async_copy(src.at[:, :, cols], dst, in_sem.at[sem_at]))
            sem_at += 1
        for src, dst in (
            (east_width, q.at[fa, c, PAD:PAD + rows]),
            (north_width, q.at[fb, c, PAD:PAD + rows]),
            (coriolis, cor.at[c]),
        ):
            here.append(pltpu.make_async_copy(src.at[:, cols], dst, in_sem.at[sem_at]))
            sem_at += 1
        for copy in here:
            copy.start()
        loads[c] = here

    lane = lax.broadcasted_iota(jnp.int32, (8, LANES), 1)
    sub = lax.broadcasted_iota(jnp.int32, (8, LANES), 0)
    first, last = lane == 0, lane == LANES - 1

    def finish_load(c):
        for copy in loads[c]:
            copy.wait()
        for l in range(levels):
            q[4 * levels + l, c, PAD:PAD + rows, :] = la[l, c].astype(jnp.float32) * th[l, c]

    finish_load(0)
    finish_load(nc - 1)
    lane_r = lax.broadcasted_iota(jnp.int32, (rows, LANES), 1)
    head = jnp.zeros((rows, LANES), jnp.float32)
    tail = jnp.zeros((rows, LANES), jnp.float32)
    for f in range(nf):
        mine = lane_r // 2 == f
        a0 = q[f, 0, PAD:PAD + rows, :]
        a1 = q[f, nc - 1, PAD:PAD + rows, :]
        head = jnp.where(mine, pltpu.roll(a0, 2 * f, 1) if f else a0, head)
        tail = jnp.where(mine, pltpu.roll(a1, 2 * f + 2, 1), tail)
    col_pack[0] = head.reshape(nb, 8, LANES)
    col_pack[1] = tail.reshape(nb, 8, LANES)
    sign_lane = jnp.where(
        jnp.logical_and(lane >= 4 * levels, lane < 8 * levels), -1.0, 1.0
    ).astype(jnp.float32)
    for side, block in ((0, head), (1, tail)):
        x = block[rows - 8:rows, :]
        y = jnp.where(lane % 2 == 0, pltpu.roll(x, LANES - 1, 1), pltpu.roll(x, 1, 1)) * sign_lane
        y = jnp.where(sub == 0, pltpu.roll(y, 2, 0), pltpu.roll(y, 4, 0))
        corner_pack[side] = jnp.where(top, y, x)

    partners = 3 + e_far.astype(jnp.int32) + w_far.astype(jnp.int32) + 3 * south.astype(jnp.int32)
    pl.semaphore_wait(barrier, partners)

    def send(src, dst, s_sem, r_sem, where):
        return pltpu.make_async_remote_copy(
            src_ref=src, dst_ref=dst, send_sem=s_sem, recv_sem=r_sem,
            device_id={"lat": where[0], "lon": where[1]}, device_id_type=pl.DeviceIdType.MESH,
        )

    to_east = send(col_pack.at[1], col_recv.at[1, 1:nb + 1], col_send.at[1], col_sem.at[1, 1], east)
    to_west = send(col_pack.at[0], col_recv.at[0, 1:nb + 1], col_send.at[0], col_sem.at[0, 1], west)
    e_side = jnp.where(top, 0, 1)
    w_side = jnp.where(top, 1, 0)
    blk = jnp.where(top, nb + 1, 0)
    which = jnp.where(top, 2, 0)
    to_ne = send(corner_pack.at[1], col_recv.at[e_side, blk], corner_send.at[0], col_sem.at[e_side, which], north_e)
    to_nw = send(corner_pack.at[0], col_recv.at[w_side, blk], corner_send.at[1], col_sem.at[w_side, which], north_w)
    to_se = send(col_pack.at[1, 0], col_recv.at[1, nb + 1], corner_send.at[2], col_sem.at[1, 2], (lat_s, east_lon))
    to_sw = send(col_pack.at[0, 0], col_recv.at[0, nb + 1], corner_send.at[3], col_sem.at[0, 2], (lat_s, west_lon))
    to_east.start()
    to_west.start()

    for c in range(1, nc - 1):
        finish_load(c)
    flip = jnp.where(top, -1.0, 1.0).astype(jnp.float32)
    for f in range(nf):
        row_pack[0, :, 2 * f:2 * f + 2, :] = q[f, 0:nc, PAD:PAD + 2, :]
        s0 = PAD + rows - 2
        near = q[f, 0:nc, s0:s0 + 1, :]
        far = jnp.where(top, q[f, 0:nc, s0 - 1:s0, :], q[f, 0:nc, s0 + 1:s0 + 2, :])
        if 2 * levels <= f < 4 * levels:
            near, far = near * flip, far * flip
        row_pack[1, :, 2 * f:2 * f + 1, :] = near
        row_pack[1, :, 2 * f + 1:2 * f + 2, :] = far

    @pl.when(top)
    def _():
        i0 = lax.broadcasted_iota(jnp.int32, (LANES, LANES), 0)
        i1 = lax.broadcasted_iota(jnp.int32, (LANES, LANES), 1)
        mirror = (i0 + i1 == LANES - 1).astype(jnp.float32)
        turned = [
            jnp.dot(row_pack[1, c, 0:2 * nf, :], mirror, precision=lax.Precision.HIGHEST,
                    preferred_element_type=jnp.float32)
            for c in range(nc)
        ]
        for c in range(nc):
            row_pack[1, nc - 1 - c, 0:2 * nf, :] = turned[c]

    slot = jnp.where(top, 1, 0)
    to_north = send(row_pack.at[1], row_recv.at[slot], row_send.at[1], row_sem.at[slot], north)
    to_south = send(row_pack.at[0], row_recv.at[1], row_send.at[0], row_sem.at[1], (lat_s, lon))
    to_north.start()

    @pl.when(south)
    def _():
        to_south.start()
        to_se.start()
        to_sw.start()

    @pl.when(e_far)
    def _():
        to_ne.start()

    @pl.when(w_far)
    def _():
        to_nw.start()

    ring = nc + 1

    def to_e(x, beside):
        return pltpu.roll(jnp.where(first, beside, x), LANES - 1, 1)

    def to_w(x, beside):
        return pltpu.roll(jnp.where(last, beside, x), 1, 1)

    def pass_a(s, c):
        cp, cm = lax.rem(c + 1, ring), lax.rem(c + ring - 1, ring)
        r0, rn, rs = pl.ds(s, 8), pl.ds(s + 1, 8), pl.ds(s - 1, 8)

        def five(f):
            x = q[f, c, r0, :]
            return (x, to_e(x, q[f, cp, r0, :]), to_w(x, q[f, cm, r0, :]), q[f, c, rn, :], q[f, c, rs, :])

        a, ae, aw, an, as_ = five(fa)
        b, be, bw, bn, bs = five(fb)
        iarea = 1.0 / (a * b)
        we, ww, wn, ws = b + be, b + bw, a + an, a + as_
        re, rw, rn_, rs_ = we / (a + ae), ww / (a + aw), wn / (b + bn), ws / (b + bs)
        k = time_step / 8.0
        we, ww, wn, ws = we * k, ww * k, wn * k, ws * k
        over = jnp.zeros_like(a)
        for l in range(levels):
            d, de, dw, dn, ds_ = five(4 * levels + l)
            inv = iarea / jnp.maximum(d, thin_floor)
            me = jnp.minimum(d, de) * inv
            mw = jnp.minimum(d, dw) * inv
            mn = jnp.minimum(d, dn) * inv
            ms = jnp.minimum(d, ds_) * inv
            ce, cw, cn, cs = me * re, mw * rw, mn * rn_, ms * rs_
            cf[l, c, r0, :] = ce
            cf[levels + l, c, r0, :] = cw
            cf[2 * levels + l, c, r0, :] = cn
            cf[3 * levels + l, c, r0, :] = cs

            def laplace(v, x, xe, xw, xn, xs):
                lap[v * levels + l, c, r0, :] = (
                    ce * (xe - x) + cw * (xw - x) + cn * (xn - x) + cs * (xs - x)
                )

            u = five(2 * levels + l)
            laplace(2, *u)
            te = me * we * (u[0] + u[1])
            tw = mw * ww * (u[0] + u[2])
            v = five(3 * levels + l)
            laplace(3, *v)
            tn = mn * wn * (v[0] + v[3])
            ts = ms * ws * (v[0] + v[4])
            tracer = []
            for i in range(2):
                x, xe, xw, xn, xs = five(i * levels + l)
                laplace(i, x, xe, xw, xn, xs)
                advect = te * (x + xe) - tw * (x + xw) + tn * (x + xn) - ts * (x + xs)
                base[i * levels + l, c, r0, :] = x - advect
                tracer.append(x)
            buoyancy = (beta_salt * tracer[1] - alpha_temp * tracer[0]) * d
            pres[l, c, r0, :] = over + 0.5 * buoyancy
            over = over + buoyancy

    def pass_b(j, c):
        cp, cm = lax.rem(c + 1, ring), lax.rem(c + ring - 1, ring)
        s = pl.multiple_of(PAD + 8 * j, 8)
        t = pl.multiple_of(8 * j, 8)
        r0, rn, rs, ro = pl.ds(s, 8), pl.ds(s + 1, 8), pl.ds(s - 1, 8), pl.ds(t, 8)
        ga = (0.5 * time_step) / q[fa, c, r0, :]
        gb = (0.5 * time_step) / q[fb, c, r0, :]
        rot = time_step * cor[c, ro, :]
        for l in range(levels):
            ce, cw = cf[l, c, r0, :], cf[levels + l, c, r0, :]
            cn, cs = cf[2 * levels + l, c, r0, :], cf[3 * levels + l, c, r0, :]
            wet = la[l, c, ro, :].astype(jnp.float32)

            def drag(v):
                f = v * levels + l
                x = lap[f, c, r0, :]
                xe, xw = to_e(x, lap[f, cp, r0, :]), to_w(x, lap[f, cm, r0, :])
                xn, xs = lap[f, c, rn, :], lap[f, c, rs, :]
                return biharm_coef * (
                    ce * (xe - x) + cw * (xw - x) + cn * (xn - x) + cs * (xs - x)
                )

            for i in range(2):
                ob[i * levels + l, c, ro, :] = wet * (base[i * levels + l, c, r0, :] - drag(i))
            p = pres[l, c, r0, :]
            ge = (to_e(p, pres[l, cp, r0, :]) - to_w(p, pres[l, cm, r0, :])) * ga
            gn = (pres[l, c, rn, :] - pres[l, c, rs, :]) * gb
            u, v = q[2 * levels + l, c, r0, :], q[3 * levels + l, c, r0, :]
            ob[2 * levels + l, c, ro, :] = wet * (u + (rot * v - ge) - drag(2))
            ob[3 * levels + l, c, ro, :] = wet * (v - (rot * u + gn) - drag(3))

    def loop(count, body):
        lax.fori_loop(0, count, lambda i, carry: (body(i), carry)[1], 0)

    def unpack_cols(block):
        s = pl.multiple_of(8 * block, 8)
        e, w = col_recv[0, block], col_recv[1, block]
        for f in range(nf):
            x = pltpu.roll(e, LANES - 2 * f, 1) if f else e
            q[f, nc, pl.ds(s, 8), :] = jnp.where(lane < 64, x, pltpu.roll(w, LANES - 2 - 2 * f, 1))

    inner = nc - 2
    loop((nb - 1) * inner, lambda i: pass_a(PAD - 1 + 8 * (1 + i // inner), 1 + lax.rem(i, inner)))
    to_east.wait_recv()
    to_west.wait_recv()
    loop(nb, lambda i: unpack_cols(i + 1))
    loop(
        (nb - 1) * 3,
        lambda i: pass_a(PAD - 1 + 8 * (1 + i // 3), lax.rem(nc - 1 + lax.rem(i, 3), ring)),
    )
    loop((nb - 2) * nc, lambda i: pass_b(1 + i // nc, lax.rem(i, nc)))

    outs = (temp_out, salt_out, uvel_out, vvel_out)
    stores = []

    def store(part, lo, size):
        for i, dst in enumerate(outs):
            for c in range(nc):
                copy = pltpu.make_async_copy(
                    ob.at[i * levels:(i + 1) * levels, c, lo:lo + size],
                    dst.at[:, lo:lo + size, c * LANES:(c + 1) * LANES],
                    out_sem.at[part, i * nc + c],
                )
                copy.start()
                stores.append(copy)

    store(0, 8, rows - 16)

    @pl.when(south)
    def _():
        send(row_pack.at[1], row_recv.at[0], row_send.at[1], row_sem.at[0], north).wait_recv()
        send(corner_pack.at[1], col_recv.at[1, 0], corner_send.at[0], col_sem.at[1, 0], east).wait_recv()
        send(corner_pack.at[0], col_recv.at[0, 0], corner_send.at[1], col_sem.at[0, 0], west).wait_recv()
        for f in range(nf):
            q[f, 0:nc, PAD - 2:PAD, :] = row_recv[0, :, 2 * f:2 * f + 2, :]
        unpack_cols(0)

    @pl.when(jnp.logical_not(south))
    def _():
        for f in range(nf):
            q[f, :, 0:PAD, :] = jnp.full((ring, PAD, LANES), 1.0 if f >= fa else 0.0, jnp.float32)

    send(row_pack.at[0], row_recv.at[1], row_send.at[0], row_sem.at[1], north).wait_recv()

    @pl.when(e_far)
    def _():
        send(corner_pack.at[1], col_recv.at[0, nb + 1], corner_send.at[0], col_sem.at[0, 2], east).wait_recv()

    @pl.when(e_self)
    def _():
        col_recv[0, nb + 1] = corner_pack[1]

    @pl.when(w_far)
    def _():
        send(corner_pack.at[0], col_recv.at[1, nb + 1], corner_send.at[1], col_sem.at[1, 2], west).wait_recv()

    @pl.when(w_self)
    def _():
        col_recv[1, nb + 1] = corner_pack[0]

    for f in range(nf):
        q[f, 0:nc, PAD + rows:PAD + rows + 2, :] = row_recv[1, :, 2 * f:2 * f + 2, :]
    unpack_cols(nb + 1)

    loop(2 * ring, lambda i: pass_a(PAD - 1 + (rows - 6) * (i // ring), lax.rem(i, ring)))
    loop(2 * nc, lambda i: pass_b((nb - 1) * (i // nc), lax.rem(i, nc)))
    store(1, 0, 8)
    store(2, rows - 8, 8)

    to_east.wait_send()
    to_west.wait_send()
    to_north.wait_send()

    @pl.when(south)
    def _():
        to_south.wait_send()
        to_se.wait_send()
        to_sw.wait_send()

    @pl.when(e_far)
    def _():
        to_ne.wait_send()

    @pl.when(w_far)
    def _():
        to_nw.wait_send()

    for copy in stores:
        copy.wait()


def shards(n_lat, n_lon, *args):
    levels, rows, width = args[0].shape
    nc, nb, nf = width // LANES, rows // 8, 5 * levels + 2
    tall = rows + 2 * PAD
    row_slots = -(-2 * nf // 8) * 8
    f32 = jnp.float32

    def plane(count):
        return pltpu.VMEM((count, nc + 1, tall, LANES), f32)

    dma = pltpu.SemaphoreType.DMA
    return pl.pallas_call(
        functools.partial(kernel, n_lat, n_lon),
        out_shape=tuple(jax.ShapeDtypeStruct((levels, rows, width), f32) for _ in range(4)),
        in_specs=[pl.BlockSpec(memory_space=pl.ANY)] * 9,
        out_specs=tuple(pl.BlockSpec(memory_space=pl.ANY) for _ in range(4)),
        scratch_shapes=[
            plane(nf),
            pltpu.VMEM((levels, nc, rows, LANES), f32),
            pltpu.VMEM((levels, nc, rows, LANES), jnp.int32),
            pltpu.VMEM((nc, rows, LANES), f32),
            plane(4 * levels),
            plane(4 * levels),
            plane(levels),
            plane(2 * levels),
            pltpu.VMEM((4 * levels, nc, rows, LANES), f32),
            pltpu.VMEM((2, nc, row_slots, LANES), f32),
            pltpu.VMEM((2, nc, row_slots, LANES), f32),
            pltpu.VMEM((2, nb, 8, LANES), f32),
            pltpu.VMEM((2, 8, LANES), f32),
            pltpu.VMEM((2, nb + 2, 8, LANES), f32),
            dma((9 * nc,)),
            dma((3, 4 * nc)),
            dma((2,)),
            dma((2,)),
            dma((2,)),
            dma((2, 3)),
            dma((4,)),
        ],
        compiler_params=pltpu.CompilerParams(
            collective_id=0, has_side_effects=True, vmem_limit_bytes=40 * 1024 * 1024
        ),
    )(*args)


def solution(mesh):
    grid, line = P(None, "lat", "lon"), P("lat", "lon")
    body = functools.partial(shards, mesh.shape["lat"], mesh.shape["lon"])
    return jax.shard_map(
        body, mesh=mesh, in_specs=(grid,) * 6 + (line,) * 3, out_specs=(grid,) * 4, check_vma=False
    )
```

```python
import functools

import jax
import jax.numpy as jnp
from jax import lax
from jax.experimental import pallas as pl
from jax.experimental.pallas import tpu as pltpu
from jax.sharding import PartitionSpec as P

time_step = 0.2
biharm_coef = 0.02
alpha_temp = 0.2
beta_salt = 0.8
thin_floor = 0.25

LANES = 128
LIMIT = 32
PAD = 8


def inverse(x):
    r = pl.reciprocal(x, approx=True)
    r = r * (2.0 - x * r)
    return r * (2.0 - x * r)


def loop(count, body):
    lax.fori_loop(0, count, lambda i, carry: (body(i), carry)[1], 0)


def edge_lanes():
    lane = lax.broadcasted_iota(jnp.int32, (8, LANES), 1)
    first, last = lane == 0, lane == LANES - 1

    def to_e(x, beside):
        return pltpu.roll(jnp.where(first, beside, x), LANES - 1, 1)

    def to_w(x, beside):
        return pltpu.roll(jnp.where(last, beside, x), 1, 1)

    return lane, to_e, to_w


def first_kernel(
    n_lat, n_lon,
    temp, salt, uvel, vvel, thick, land, east_width, north_width,
    q, la, lap, cf, pres, base,
    th, row_pack, row_recv, col_pack, corner_pack, col_recv,
    in_sem, row_send, row_sem, col_send, col_sem, corner_send,
):
    levels, rows, width = temp.shape
    nc = width // LANES
    nb = rows // 8
    nf = 5 * levels + 2
    fa, fb = 5 * levels, 5 * levels + 1
    lat, lon = lax.axis_index("lat"), lax.axis_index("lon")
    top = lat == n_lat - 1
    south = lat > 0
    east_lon = lax.rem(lon + 1, n_lon)
    west_lon = lax.rem(lon + n_lon - 1, n_lon)
    lat_n = jnp.where(top, lat, lat + 1)
    lat_s = jnp.where(south, lat - 1, 0)
    north = (lat_n, jnp.where(top, n_lon - 1 - lon, lon))
    fold_e = lax.rem(2 * n_lon - 2 - lon, n_lon)
    fold_w = lax.rem(n_lon - lon, n_lon)
    north_e = (lat_n, jnp.where(top, fold_e, east_lon))
    north_w = (lat_n, jnp.where(top, fold_w, west_lon))
    e_self = jnp.logical_and(top, fold_e == lon)
    w_self = jnp.logical_and(top, fold_w == lon)
    e_far, w_far = jnp.logical_not(e_self), jnp.logical_not(w_self)
    east, west = (lat, east_lon), (lat, west_lon)

    barrier = pltpu.get_barrier_semaphore()

    def greet(where):
        pl.semaphore_signal(barrier, inc=1, device_id={"lat": where[0], "lon": where[1]}, device_id_type=pl.DeviceIdType.MESH)

    greet(east)
    greet(west)
    greet(north)

    @pl.when(e_far)
    def _():
        greet(north_e)

    @pl.when(w_far)
    def _():
        greet(north_w)

    @pl.when(south)
    def _():
        greet((lat_s, lon))
        greet((lat_s, east_lon))
        greet((lat_s, west_lon))

    order = [0, nc - 1] + list(range(1, nc - 1))
    loads = {}
    sem_at = 0
    for c in order:
        cols = pl.ds(c * LANES, LANES)
        here = []
        for src, dst in (
            (land, la.at[:, c]),
            (thick, th.at[:, c]),
            (temp, q.at[0:levels, c, PAD:PAD + rows]),
            (salt, q.at[levels:2 * levels, c, PAD:PAD + rows]),
            (uvel, q.at[2 * levels:3 * levels, c, PAD:PAD + rows]),
            (vvel, q.at[3 * levels:4 * levels, c, PAD:PAD + rows]),
        ):
            here.append(pltpu.make_async_copy(src.at[:, :, cols], dst, in_sem.at[sem_at]))
            sem_at += 1
        for src, dst in (
            (east_width, q.at[fa, c, PAD:PAD + rows]),
            (north_width, q.at[fb, c, PAD:PAD + rows]),
        ):
            here.append(pltpu.make_async_copy(src.at[:, cols], dst, in_sem.at[sem_at]))
            sem_at += 1
        for copy in here:
            copy.start()
        loads[c] = here

    lane, to_e, to_w = edge_lanes()
    sub = lax.broadcasted_iota(jnp.int32, (8, LANES), 0)

    def finish_load(c):
        for copy in loads[c]:
            copy.wait()
        for l in range(levels):
            q[4 * levels + l, c, PAD:PAD + rows, :] = la[l, c].astype(jnp.float32) * th[l, c]

    finish_load(0)
    finish_load(nc - 1)
    lane_r = lax.broadcasted_iota(jnp.int32, (rows, LANES), 1)
    head = jnp.zeros((rows, LANES), jnp.float32)
    tail = jnp.zeros((rows, LANES), jnp.float32)
    for f in range(nf):
        mine = lane_r // 2 == f
        a0 = q[f, 0, PAD:PAD + rows, :]
        a1 = q[f, nc - 1, PAD:PAD + rows, :]
        head = jnp.where(mine, pltpu.roll(a0, 2 * f, 1) if f else a0, head)
        tail = jnp.where(mine, pltpu.roll(a1, 2 * f + 2, 1), tail)
    col_pack[0] = head.reshape(nb, 8, LANES)
    col_pack[1] = tail.reshape(nb, 8, LANES)
    sign_lane = jnp.where(
        jnp.logical_and(lane >= 4 * levels, lane < 8 * levels), -1.0, 1.0
    ).astype(jnp.float32)
    for side, block in ((0, head), (1, tail)):
        x = block[rows - 8:rows, :]
        y = jnp.where(lane % 2 == 0, pltpu.roll(x, LANES - 1, 1), pltpu.roll(x, 1, 1)) * sign_lane
        y = jnp.where(sub == 0, pltpu.roll(y, 2, 0), pltpu.roll(y, 4, 0))
        corner_pack[side] = jnp.where(top, y, x)

    partners = 3 + e_far.astype(jnp.int32) + w_far.astype(jnp.int32) + 3 * south.astype(jnp.int32)
    pl.semaphore_wait(barrier, partners)

    def send(src, dst, s_sem, r_sem, where):
        return pltpu.make_async_remote_copy(
            src_ref=src, dst_ref=dst, send_sem=s_sem, recv_sem=r_sem,
            device_id={"lat": where[0], "lon": where[1]}, device_id_type=pl.DeviceIdType.MESH,
        )

    to_east = send(col_pack.at[1], col_recv.at[1, 1:nb + 1], col_send.at[1], col_sem.at[1, 1], east)
    to_west = send(col_pack.at[0], col_recv.at[0, 1:nb + 1], col_send.at[0], col_sem.at[0, 1], west)
    e_side = jnp.where(top, 0, 1)
    w_side = jnp.where(top, 1, 0)
    blk = jnp.where(top, nb + 1, 0)
    which = jnp.where(top, 2, 0)
    to_ne = send(corner_pack.at[1], col_recv.at[e_side, blk], corner_send.at[0], col_sem.at[e_side, which], north_e)
    to_nw = send(corner_pack.at[0], col_recv.at[w_side, blk], corner_send.at[1], col_sem.at[w_side, which], north_w)
    to_se = send(col_pack.at[1, 0], col_recv.at[1, nb + 1], corner_send.at[2], col_sem.at[1, 2], (lat_s, east_lon))
    to_sw = send(col_pack.at[0, 0], col_recv.at[0, nb + 1], corner_send.at[3], col_sem.at[0, 2], (lat_s, west_lon))
    to_east.start()
    to_west.start()

    for c in range(1, nc - 1):
        finish_load(c)
    flip = jnp.where(top, -1.0, 1.0).astype(jnp.float32)
    for f in range(nf):
        row_pack[0, :, 2 * f:2 * f + 2, :] = q[f, 0:nc, PAD:PAD + 2, :]
        s0 = PAD + rows - 2
        near = q[f, 0:nc, s0:s0 + 1, :]
        far = jnp.where(top, q[f, 0:nc, s0 - 1:s0, :], q[f, 0:nc, s0 + 1:s0 + 2, :])
        if 2 * levels <= f < 4 * levels:
            near, far = near * flip, far * flip
        row_pack[1, :, 2 * f:2 * f + 1, :] = near
        row_pack[1, :, 2 * f + 1:2 * f + 2, :] = far

    @pl.when(top)
    def _():
        i0 = lax.broadcasted_iota(jnp.int32, (LANES, LANES), 0)
        i1 = lax.broadcasted_iota(jnp.int32, (LANES, LANES), 1)
        mirror = (i0 + i1 == LANES - 1).astype(jnp.float32)
        turned = [
            jnp.dot(row_pack[1, c, 0:2 * nf, :], mirror, precision=lax.Precision.HIGHEST,
                    preferred_element_type=jnp.float32)
            for c in range(nc)
        ]
        for c in range(nc):
            row_pack[1, nc - 1 - c, 0:2 * nf, :] = turned[c]

    slot = jnp.where(top, 1, 0)
    to_north = send(row_pack.at[1], row_recv.at[slot], row_send.at[1], row_sem.at[slot], north)
    to_south = send(row_pack.at[0], row_recv.at[1], row_send.at[0], row_sem.at[1], (lat_s, lon))
    to_north.start()

    @pl.when(south)
    def _():
        to_south.start()
        to_se.start()
        to_sw.start()

    @pl.when(e_far)
    def _():
        to_ne.start()

    @pl.when(w_far)
    def _():
        to_nw.start()

    ring = nc + 1

    def pass_a(s, c):
        cp, cm = (c + 1) % ring, (c - 1) % ring
        r0, rn, rs = pl.ds(s, 8), pl.ds(s + 1, 8), pl.ds(s - 1, 8)

        def five(f):
            x = q[f, c, r0, :]
            return (x, to_e(x, q[f, cp, r0, :]), to_w(x, q[f, cm, r0, :]), q[f, c, rn, :], q[f, c, rs, :])

        a, ae, aw, an, as_ = five(fa)
        b, be, bw, bn, bs = five(fb)
        iarea = inverse(a * b)
        we, ww, wn, ws = b + be, b + bw, a + an, a + as_
        re, rw = we * inverse(a + ae), ww * inverse(a + aw)
        rn_, rs_ = wn * inverse(b + bn), ws * inverse(b + bs)
        k = time_step / 8.0
        we, ww, wn, ws = we * k, ww * k, wn * k, ws * k
        over = jnp.zeros_like(a)
        for l in range(levels):
            d, de, dw, dn, ds_ = five(4 * levels + l)
            inv = iarea * inverse(jnp.maximum(d, thin_floor))
            me = jnp.minimum(d, de) * inv
            mw = jnp.minimum(d, dw) * inv
            mn = jnp.minimum(d, dn) * inv
            ms = jnp.minimum(d, ds_) * inv
            ce, cw, cn, cs = me * re, mw * rw, mn * rn_, ms * rs_
            cf[l, c, r0, :] = ce
            cf[levels + l, c, r0, :] = cw
            cf[2 * levels + l, c, r0, :] = cn
            cf[3 * levels + l, c, r0, :] = cs

            def laplace(v, x, xe, xw, xn, xs):
                lap[v * levels + l, c, r0, :] = (
                    ce * (xe - x) + cw * (xw - x) + cn * (xn - x) + cs * (xs - x)
                )

            u = five(2 * levels + l)
            laplace(2, *u)
            te = me * we * (u[0] + u[1])
            tw = mw * ww * (u[0] + u[2])
            v = five(3 * levels + l)
            laplace(3, *v)
            tn = mn * wn * (v[0] + v[3])
            ts = ms * ws * (v[0] + v[4])
            tracer = []
            for i in range(2):
                x, xe, xw, xn, xs = five(i * levels + l)
                laplace(i, x, xe, xw, xn, xs)
                advect = te * (x + xe) - tw * (x + xw) + tn * (x + xn) - ts * (x + xs)
                base[i * levels + l, c, r0, :] = x - advect
                tracer.append(x)
            buoyancy = (beta_salt * tracer[1] - alpha_temp * tracer[0]) * d
            pres[l, c, r0, :] = over + 0.5 * buoyancy
            over = over + buoyancy

    def unpack_cols(block):
        s = pl.multiple_of(8 * block, 8)
        e, w = col_recv[0, block], col_recv[1, block]
        for f in range(nf):
            x = pltpu.roll(e, LANES - 2 * f, 1) if f else e
            q[f, nc, pl.ds(s, 8), :] = jnp.where(lane < 64, x, pltpu.roll(w, LANES - 2 - 2 * f, 1))

    def row_a(s, tiles):
        for c in tiles:
            pass_a(s, c)

    def unpack_cols(block):
        s = pl.multiple_of(8 * block, 8)
        e, w = col_recv[0, block], col_recv[1, block]
        for f in range(nf):
            x = pltpu.roll(e, LANES - 2 * f, 1) if f else e
            q[f, nc, pl.ds(s, 8), :] = jnp.where(lane < 64, x, pltpu.roll(w, LANES - 2 - 2 * f, 1))

    def row_a(s, tiles):
        for c in tiles:
            pass_a(s, c)

    def row_b(j):
        for c in range(nc):
            pass_b(j, c)

    loop(nb - 1, lambda k: row_a(PAD - 1 + 8 * (1 + k), range(1, nc - 1)))
    to_east.wait_recv()
    to_west.wait_recv()
    loop(nb, lambda i: unpack_cols(i + 1))
    loop(nb - 1, lambda k: row_a(PAD - 1 + 8 * (1 + k), (nc - 1, nc, 0)))

    @pl.when(south)
    def _():
        send(row_pack.at[1], row_recv.at[0], row_send.at[1], row_sem.at[0], north).wait_recv()
        send(corner_pack.at[1], col_recv.at[1, 0], corner_send.at[0], col_sem.at[1, 0], east).wait_recv()
        send(corner_pack.at[0], col_recv.at[0, 0], corner_send.at[1], col_sem.at[0, 0], west).wait_recv()
        for f in range(nf):
            q[f, 0:nc, PAD - 2:PAD, :] = row_recv[0, :, 2 * f:2 * f + 2, :]
        unpack_cols(0)

    @pl.when(jnp.logical_not(south))
    def _():
        for f in range(nf):
            q[f, :, 0:PAD, :] = jnp.full((ring, PAD, LANES), 1.0 if f >= fa else 0.0, jnp.float32)

    send(row_pack.at[0], row_recv.at[1], row_send.at[0], row_sem.at[1], north).wait_recv()

    @pl.when(e_far)
    def _():
        send(corner_pack.at[1], col_recv.at[0, nb + 1], corner_send.at[0], col_sem.at[0, 2], east).wait_recv()

    @pl.when(e_self)
    def _():
        col_recv[0, nb + 1] = corner_pack[1]

    @pl.when(w_far)
    def _():
        send(corner_pack.at[0], col_recv.at[1, nb + 1], corner_send.at[1], col_sem.at[1, 2], west).wait_recv()

    @pl.when(w_self)
    def _():
        col_recv[1, nb + 1] = corner_pack[0]

    for f in range(nf):
        q[f, 0:nc, PAD + rows:PAD + rows + 2, :] = row_recv[1, :, 2 * f:2 * f + 2, :]
    unpack_cols(nb + 1)

    loop(2, lambda i: row_a(PAD - 1 + (rows - 6) * i, range(ring)))

    to_east.wait_send()
    to_west.wait_send()
    to_north.wait_send()

    @pl.when(south)
    def _():
        to_south.wait_send()
        to_se.wait_send()
        to_sw.wait_send()

    @pl.when(e_far)
    def _():
        to_ne.wait_send()

    @pl.when(w_far)
    def _():
        to_nw.wait_send()


def second_kernel(
    coriolis, q, la, lap, cf, pres, base, temp_out, salt_out, uvel_out, vvel_out,
    cor, ob, cor_sem, out_sem,
):
    levels, rows, width = temp_out.shape
    nc, nb = width // LANES, rows // 8
    fa, fb = 5 * levels, 5 * levels + 1
    ring = nc + 1
    loads = []
    for c in range(nc):
        copy = pltpu.make_async_copy(
            coriolis.at[:, c * LANES:(c + 1) * LANES], cor.at[c], cor_sem.at[c]
        )
        copy.start()
        loads.append(copy)
    lane, to_e, to_w = edge_lanes()

    def pass_b(j, c):
        cp, cm = (c + 1) % ring, (c - 1) % ring
        s = pl.multiple_of(PAD + 8 * j, 8)
        t = pl.multiple_of(8 * j, 8)
        r0, rn, rs, ro = pl.ds(s, 8), pl.ds(s + 1, 8), pl.ds(s - 1, 8), pl.ds(t, 8)
        ga = (0.5 * time_step) * inverse(q[fa, c, r0, :])
        gb = (0.5 * time_step) * inverse(q[fb, c, r0, :])
        rot = time_step * cor[c, ro, :]
        for l in range(levels):
            ce, cw = cf[l, c, r0, :], cf[levels + l, c, r0, :]
            cn, cs = cf[2 * levels + l, c, r0, :], cf[3 * levels + l, c, r0, :]
            wet = la[l, c, ro, :].astype(jnp.float32)

            def drag(v):
                f = v * levels + l
                x = lap[f, c, r0, :]
                xe, xw = to_e(x, lap[f, cp, r0, :]), to_w(x, lap[f, cm, r0, :])
                xn, xs = lap[f, c, rn, :], lap[f, c, rs, :]
                return biharm_coef * (
                    ce * (xe - x) + cw * (xw - x) + cn * (xn - x) + cs * (xs - x)
                )

            for i in range(2):
                ob[i * levels + l, c, ro, :] = wet * (base[i * levels + l, c, r0, :] - drag(i))
            p = pres[l, c, r0, :]
            ge = (to_e(p, pres[l, cp, r0, :]) - to_w(p, pres[l, cm, r0, :])) * ga
            gn = (pres[l, c, rn, :] - pres[l, c, rs, :]) * gb
            u, v = q[2 * levels + l, c, r0, :], q[3 * levels + l, c, r0, :]
            ob[2 * levels + l, c, ro, :] = wet * (u + (rot * v - ge) - drag(2))
            ob[3 * levels + l, c, ro, :] = wet * (v - (rot * u + gn) - drag(3))

    for copy in loads:
        copy.wait()
    outs = (temp_out, salt_out, uvel_out, vvel_out)

    def row_b(j):
        for c in range(nc):
            pass_b(j, c)

    stores = []
    for part in range(2):
        lo = part * (rows // 2)
        loop(nb // 2, lambda j: row_b(part * (nb // 2) + j))
        for i, dst in enumerate(outs):
            for c in range(nc):
                copy = pltpu.make_async_copy(
                    ob.at[i * levels:(i + 1) * levels, c, lo:lo + rows // 2],
                    dst.at[:, lo:lo + rows // 2, c * LANES:(c + 1) * LANES],
                    out_sem.at[part, i * nc + c],
                )
                copy.start()
                stores.append(copy)
    for copy in stores:
        copy.wait()


def shards(n_lat, n_lon, *args):
    levels, rows, width = args[0].shape
    nc, nb, nf = width // LANES, rows // 8, 5 * levels + 2
    tall = rows + 2 * PAD
    row_slots = -(-2 * nf // 8) * 8
    f32 = jnp.float32

    def plane(count):
        return pltpu.VMEM((count, nc + 1, tall, LANES), f32)

    dma = pltpu.SemaphoreType.DMA
    held = pl.BlockSpec(memory_space=pltpu.VMEM)
    far = pl.BlockSpec(memory_space=pl.ANY)
    args = [pltpu.with_memory_space_constraint(x, pltpu.HBM) for x in args]
    middle = pl.pallas_call(
        functools.partial(first_kernel, n_lat, n_lon),
        out_shape=(
            plane(nf),
            pltpu.VMEM((levels, nc, rows, LANES), jnp.int32),
            plane(4 * levels),
            plane(4 * levels),
            plane(levels),
            plane(2 * levels),
        ),
        in_specs=[far] * 8,
        out_specs=(held,) * 6,
        scratch_shapes=[
            pltpu.VMEM((levels, nc, rows, LANES), f32),
            pltpu.VMEM((2, nc, row_slots, LANES), f32),
            pltpu.VMEM((2, nc, row_slots, LANES), f32),
            pltpu.VMEM((2, nb, 8, LANES), f32),
            pltpu.VMEM((2, 8, LANES), f32),
            pltpu.VMEM((2, nb + 2, 8, LANES), f32),
            dma((8 * nc,)),
            dma((2,)),
            dma((2,)),
            dma((2,)),
            dma((2, 3)),
            dma((4,)),
        ],
        compiler_params=pltpu.CompilerParams(
            collective_id=0, has_side_effects=True, vmem_limit_bytes=LIMIT * 1024 * 1024
        ),
    )(*args[:8])
    return pl.pallas_call(
        second_kernel,
        out_shape=tuple(jax.ShapeDtypeStruct((levels, rows, width), f32) for _ in range(4)),
        in_specs=[far] + [held] * 6,
        out_specs=(far,) * 4,
        scratch_shapes=[
            pltpu.VMEM((nc, rows, LANES), f32),
            pltpu.VMEM((4 * levels, nc, rows, LANES), f32),
            dma((nc,)),
            dma((2, 4 * nc)),
        ],
        compiler_params=pltpu.CompilerParams(vmem_limit_bytes=LIMIT * 1024 * 1024),
    )(args[8], *middle)


def solution(mesh):
    grid, line = P(None, "lat", "lon"), P("lat", "lon")
    body = functools.partial(shards, mesh.shape["lat"], mesh.shape["lon"])
    return jax.shard_map(
        body, mesh=mesh, in_specs=(grid,) * 6 + (line,) * 3, out_specs=(grid,) * 4, check_vma=False
    )
```

```python
import functools

import jax
import jax.numpy as jnp
from jax import lax
from jax.experimental import pallas as pl
from jax.experimental.pallas import tpu as pltpu
from jax.sharding import PartitionSpec as P

time_step = 0.2
biharm_coef = 0.02
alpha_temp = 0.2
beta_salt = 0.8
thin_floor = 0.25

LANES = 128
LIMIT = 32
PARTS = 4
PAD = 8


def inverse(x):
    return pl.reciprocal(x, approx=True)


def loop(count, body):
    lax.fori_loop(0, count, lambda i, carry: (body(i), carry)[1], 0)


def edge_lanes():
    lane = lax.broadcasted_iota(jnp.int32, (8, LANES), 1)
    first, last = lane == 0, lane == LANES - 1

    def to_e(x, beside):
        return pltpu.roll(jnp.where(first, beside, x), LANES - 1, 1)

    def to_w(x, beside):
        return pltpu.roll(jnp.where(last, beside, x), 1, 1)

    return lane, to_e, to_w


def first_kernel(
    n_lat, n_lon,
    temp, salt, uvel, vvel, thick, land, east_width, north_width, coriolis,
    q, la, cor, lap, cf, pres, base,
    th, edge, edge_land, row_pack, row_recv, col_pack, corner_pack, col_recv,
    edge_sem, in_sem, row_send, row_sem, col_send, col_sem, corner_send,
):
    levels, rows, width = temp.shape
    nc = width // LANES
    nb = rows // 8
    nf = 5 * levels + 2
    fa, fb = 5 * levels, 5 * levels + 1
    lat, lon = lax.axis_index("lat"), lax.axis_index("lon")
    top = lat == n_lat - 1
    south = lat > 0
    east_lon = lax.rem(lon + 1, n_lon)
    west_lon = lax.rem(lon + n_lon - 1, n_lon)
    lat_n = jnp.where(top, lat, lat + 1)
    lat_s = jnp.where(south, lat - 1, 0)
    north = (lat_n, jnp.where(top, n_lon - 1 - lon, lon))
    fold_e = lax.rem(2 * n_lon - 2 - lon, n_lon)
    fold_w = lax.rem(n_lon - lon, n_lon)
    north_e = (lat_n, jnp.where(top, fold_e, east_lon))
    north_w = (lat_n, jnp.where(top, fold_w, west_lon))
    e_self = jnp.logical_and(top, fold_e == lon)
    w_self = jnp.logical_and(top, fold_w == lon)
    e_far, w_far = jnp.logical_not(e_self), jnp.logical_not(w_self)
    east, west = (lat, east_lon), (lat, west_lon)

    barrier = pltpu.get_barrier_semaphore()

    def greet(where):
        pl.semaphore_signal(barrier, inc=1, device_id={"lat": where[0], "lon": where[1]}, device_id_type=pl.DeviceIdType.MESH)

    greet(east)
    greet(west)
    greet(north)

    @pl.when(e_far)
    def _():
        greet(north_e)

    @pl.when(w_far)
    def _():
        greet(north_w)

    @pl.when(south)
    def _():
        greet((lat_s, lon))
        greet((lat_s, east_lon))
        greet((lat_s, west_lon))

    edge_loads = []
    for side, lo in ((0, 0), (1, rows - 8)):
        for i, (src, dst) in enumerate((
            (land, edge_land.at[side]),
            (thick, edge.at[side, 4 * levels:5 * levels]),
            (temp, edge.at[side, 0:levels]),
            (salt, edge.at[side, levels:2 * levels]),
            (uvel, edge.at[side, 2 * levels:3 * levels]),
            (vvel, edge.at[side, 3 * levels:4 * levels]),
            (east_width, edge.at[side, fa]),
            (north_width, edge.at[side, fb]),
        )):
            part = src.at[:, lo:lo + 8] if i < 6 else src.at[lo:lo + 8]
            copy = pltpu.make_async_copy(part, dst, edge_sem.at[8 * side + i])
            copy.start()
            edge_loads.append(copy)
    order = [0, nc - 1] + list(range(1, nc - 1))
    loads = {}
    sem_at = 0
    for c in order:
        cols = pl.ds(c * LANES, LANES)
        here = []
        for src, dst in (
            (land, la.at[:, c]),
            (thick, th.at[:, c]),
            (temp, q.at[0:levels, c, PAD:PAD + rows]),
            (salt, q.at[levels:2 * levels, c, PAD:PAD + rows]),
            (uvel, q.at[2 * levels:3 * levels, c, PAD:PAD + rows]),
            (vvel, q.at[3 * levels:4 * levels, c, PAD:PAD + rows]),
        ):
            here.append(pltpu.make_async_copy(src.at[:, :, cols], dst, in_sem.at[sem_at]))
            sem_at += 1
        for src, dst in (
            (east_width, q.at[fa, c, PAD:PAD + rows]),
            (north_width, q.at[fb, c, PAD:PAD + rows]),
            (coriolis, cor.at[c]),
        ):
            here.append(pltpu.make_async_copy(src.at[:, cols], dst, in_sem.at[sem_at]))
            sem_at += 1
        for copy in here:
            copy.start()
        loads[c] = here

    lane, to_e, to_w = edge_lanes()
    sub = lax.broadcasted_iota(jnp.int32, (8, LANES), 0)

    def finish_load(c):
        for copy in loads[c]:
            copy.wait()
        for l in range(levels):
            q[4 * levels + l, c, PAD:PAD + rows, :] = la[l, c].astype(jnp.float32) * th[l, c]

    for copy in edge_loads:
        copy.wait()
    flip = jnp.where(top, -1.0, 1.0).astype(jnp.float32)
    for side in range(2):
        for l in range(levels):
            f = 4 * levels + l
            edge[side, f] = edge_land[side, l].astype(jnp.float32) * edge[side, f]
    for f in range(nf):
        for c in range(nc):
            cols = slice(c * LANES, (c + 1) * LANES)
            row_pack[0, c, 2 * f:2 * f + 2, :] = edge[0, f, 0:2, cols]
            near = edge[1, f, 6:7, cols]
            far = jnp.where(top, edge[1, f, 5:6, cols], edge[1, f, 7:8, cols])
            if 2 * levels <= f < 4 * levels:
                near, far = near * flip, far * flip
            row_pack[1, c, 2 * f:2 * f + 1, :] = near
            row_pack[1, c, 2 * f + 1:2 * f + 2, :] = far

    @pl.when(top)
    def _():
        i0 = lax.broadcasted_iota(jnp.int32, (LANES, LANES), 0)
        i1 = lax.broadcasted_iota(jnp.int32, (LANES, LANES), 1)
        mirror = (i0 + i1 == LANES - 1).astype(jnp.float32)
        turned = [
            jnp.dot(row_pack[1, c, 0:2 * nf, :], mirror, precision=lax.Precision.HIGHEST,
                    preferred_element_type=jnp.float32)
            for c in range(nc)
        ]
        for c in range(nc):
            row_pack[1, nc - 1 - c, 0:2 * nf, :] = turned[c]

    partners = 3 + e_far.astype(jnp.int32) + w_far.astype(jnp.int32) + 3 * south.astype(jnp.int32)
    pl.semaphore_wait(barrier, partners)

    def send(src, dst, s_sem, r_sem, where):
        return pltpu.make_async_remote_copy(
            src_ref=src, dst_ref=dst, send_sem=s_sem, recv_sem=r_sem,
            device_id={"lat": where[0], "lon": where[1]}, device_id_type=pl.DeviceIdType.MESH,
        )

    slot = jnp.where(top, 1, 0)
    to_north = send(row_pack.at[1], row_recv.at[slot], row_send.at[1], row_sem.at[slot], north)
    to_south = send(row_pack.at[0], row_recv.at[1], row_send.at[0], row_sem.at[1], (lat_s, lon))
    to_north.start()

    @pl.when(south)
    def _():
        to_south.start()

    finish_load(0)
    finish_load(nc - 1)
    lane_r = lax.broadcasted_iota(jnp.int32, (rows, LANES), 1)
    head = jnp.zeros((rows, LANES), jnp.float32)
    tail = jnp.zeros((rows, LANES), jnp.float32)
    for f in range(nf):
        mine = lane_r // 2 == f
        a0 = q[f, 0, PAD:PAD + rows, :]
        a1 = q[f, nc - 1, PAD:PAD + rows, :]
        head = jnp.where(mine, pltpu.roll(a0, 2 * f, 1) if f else a0, head)
        tail = jnp.where(mine, pltpu.roll(a1, 2 * f + 2, 1), tail)
    col_pack[0] = head.reshape(nb, 8, LANES)
    col_pack[1] = tail.reshape(nb, 8, LANES)
    sign_lane = jnp.where(
        jnp.logical_and(lane >= 4 * levels, lane < 8 * levels), -1.0, 1.0
    ).astype(jnp.float32)
    for side, block in ((0, head), (1, tail)):
        x = block[rows - 8:rows, :]
        y = jnp.where(lane % 2 == 0, pltpu.roll(x, LANES - 1, 1), pltpu.roll(x, 1, 1)) * sign_lane
        y = jnp.where(sub == 0, pltpu.roll(y, 2, 0), pltpu.roll(y, 4, 0))
        corner_pack[side] = jnp.where(top, y, x)

    to_east = send(col_pack.at[1], col_recv.at[1, 1:nb + 1], col_send.at[1], col_sem.at[1, 1], east)
    to_west = send(col_pack.at[0], col_recv.at[0, 1:nb + 1], col_send.at[0], col_sem.at[0, 1], west)
    e_side = jnp.where(top, 0, 1)
    w_side = jnp.where(top, 1, 0)
    blk = jnp.where(top, nb + 1, 0)
    which = jnp.where(top, 2, 0)
    to_ne = send(corner_pack.at[1], col_recv.at[e_side, blk], corner_send.at[0], col_sem.at[e_side, which], north_e)
    to_nw = send(corner_pack.at[0], col_recv.at[w_side, blk], corner_send.at[1], col_sem.at[w_side, which], north_w)
    to_se = send(col_pack.at[1, 0], col_recv.at[1, nb + 1], corner_send.at[2], col_sem.at[1, 2], (lat_s, east_lon))
    to_sw = send(col_pack.at[0, 0], col_recv.at[0, nb + 1], corner_send.at[3], col_sem.at[0, 2], (lat_s, west_lon))
    to_east.start()
    to_west.start()

    @pl.when(south)
    def _():
        to_se.start()
        to_sw.start()

    @pl.when(e_far)
    def _():
        to_ne.start()

    @pl.when(w_far)
    def _():
        to_nw.start()

    for c in range(1, nc - 1):
        finish_load(c)
    ring = nc + 1

    def pass_a(s, c):
        cp, cm = (c + 1) % ring, (c - 1) % ring
        r0, rn, rs = pl.ds(s, 8), pl.ds(s + 1, 8), pl.ds(s - 1, 8)

        def five(f):
            x = q[f, c, r0, :]
            return (x, to_e(x, q[f, cp, r0, :]), to_w(x, q[f, cm, r0, :]), q[f, c, rn, :], q[f, c, rs, :])

        a, ae, aw, an, as_ = five(fa)
        b, be, bw, bn, bs = five(fb)
        area = a * b
        root = biharm_coef ** 0.5
        we, ww, wn, ws = b + be, b + bw, a + an, a + as_
        re, rw = (root * we) * inverse(a + ae), (root * ww) * inverse(a + aw)
        rn_, rs_ = (root * wn) * inverse(b + bn), (root * ws) * inverse(b + bs)
        k = time_step / 8.0
        we, ww, wn, ws = we * k, ww * k, wn * k, ws * k
        over = jnp.zeros_like(a)
        for l in range(levels):
            d, de, dw, dn, ds_ = five(4 * levels + l)
            inv = inverse(area * jnp.maximum(d, thin_floor))
            me = jnp.minimum(d, de) * inv
            mw = jnp.minimum(d, dw) * inv
            mn = jnp.minimum(d, dn) * inv
            ms = jnp.minimum(d, ds_) * inv
            ce, cw, cn, cs = me * re, mw * rw, mn * rn_, ms * rs_
            if c < nc:
                cf[l, c, r0, :] = ce
                cf[levels + l, c, r0, :] = cw
                cf[2 * levels + l, c, r0, :] = cn
                cf[3 * levels + l, c, r0, :] = cs

            def laplace(v, x, xe, xw, xn, xs):
                lap[v * levels + l, c, r0, :] = (
                    ce * (xe - x) + cw * (xw - x) + cn * (xn - x) + cs * (xs - x)
                )

            u = five(2 * levels + l)
            laplace(2, *u)
            te = me * we * (u[0] + u[1])
            tw = mw * ww * (u[0] + u[2])
            v = five(3 * levels + l)
            laplace(3, *v)
            tn = mn * wn * (v[0] + v[3])
            ts = ms * ws * (v[0] + v[4])
            tracer = []
            for i in range(2):
                x, xe, xw, xn, xs = five(i * levels + l)
                laplace(i, x, xe, xw, xn, xs)
                if c < nc:
                    advect = te * (x + xe) - tw * (x + xw) + tn * (x + xn) - ts * (x + xs)
                    base[i * levels + l, c, r0, :] = x - advect
                tracer.append(x)
            buoyancy = (beta_salt * tracer[1] - alpha_temp * tracer[0]) * d
            pres[l, c, r0, :] = over + 0.5 * buoyancy
            over = over + buoyancy

    def row_a(s, tiles):
        for c in tiles:
            pass_a(s, c)

    def unpack_cols(block):
        s = pl.multiple_of(8 * block, 8)
        e, w = col_recv[0, block], col_recv[1, block]
        for f in range(nf):
            x = pltpu.roll(e, LANES - 2 * f, 1) if f else e
            q[f, nc, pl.ds(s, 8), :] = jnp.where(lane < 64, x, pltpu.roll(w, LANES - 2 - 2 * f, 1))

    def row_a(s, tiles):
        for c in tiles:
            pass_a(s, c)

    def row_b(j):
        for c in range(nc):
            pass_b(j, c)

    loop(nb - 1, lambda k: row_a(PAD - 1 + 8 * (1 + k), range(1, nc - 1)))
    to_east.wait_recv()
    to_west.wait_recv()
    loop(nb, lambda i: unpack_cols(i + 1))
    loop(nb - 1, lambda k: row_a(PAD - 1 + 8 * (1 + k), (nc - 1, nc, 0)))

    @pl.when(south)
    def _():
        send(row_pack.at[1], row_recv.at[0], row_send.at[1], row_sem.at[0], north).wait_recv()
        send(corner_pack.at[1], col_recv.at[1, 0], corner_send.at[0], col_sem.at[1, 0], east).wait_recv()
        send(corner_pack.at[0], col_recv.at[0, 0], corner_send.at[1], col_sem.at[0, 0], west).wait_recv()
        for f in range(nf):
            q[f, 0:nc, PAD - 2:PAD, :] = row_recv[0, :, 2 * f:2 * f + 2, :]
        unpack_cols(0)

    @pl.when(jnp.logical_not(south))
    def _():
        for f in range(nf):
            q[f, :, 0:PAD, :] = jnp.full((ring, PAD, LANES), 1.0 if f >= fa else 0.0, jnp.float32)

    send(row_pack.at[0], row_recv.at[1], row_send.at[0], row_sem.at[1], north).wait_recv()

    @pl.when(e_far)
    def _():
        send(corner_pack.at[1], col_recv.at[0, nb + 1], corner_send.at[0], col_sem.at[0, 2], east).wait_recv()

    @pl.when(e_self)
    def _():
        col_recv[0, nb + 1] = corner_pack[1]

    @pl.when(w_far)
    def _():
        send(corner_pack.at[0], col_recv.at[1, nb + 1], corner_send.at[1], col_sem.at[1, 2], west).wait_recv()

    @pl.when(w_self)
    def _():
        col_recv[1, nb + 1] = corner_pack[0]

    for f in range(nf):
        q[f, 0:nc, PAD + rows:PAD + rows + 2, :] = row_recv[1, :, 2 * f:2 * f + 2, :]
    unpack_cols(nb + 1)

    loop(2, lambda i: row_a(PAD - 1 + (rows - 6) * i, range(ring)))

    to_east.wait_send()
    to_west.wait_send()
    to_north.wait_send()

    @pl.when(south)
    def _():
        to_south.wait_send()
        to_se.wait_send()
        to_sw.wait_send()

    @pl.when(e_far)
    def _():
        to_ne.wait_send()

    @pl.when(w_far)
    def _():
        to_nw.wait_send()


def second_kernel(
    q, la, cor, lap, cf, pres, base, temp_out, salt_out, uvel_out, vvel_out,
    ob, out_sem,
):
    levels, rows, width = temp_out.shape
    nc, nb = width // LANES, rows // 8
    fa, fb = 5 * levels, 5 * levels + 1
    ring = nc + 1
    lane, to_e, to_w = edge_lanes()

    def pass_b(j, c):
        cp, cm = (c + 1) % ring, (c - 1) % ring
        s = pl.multiple_of(PAD + 8 * j, 8)
        t = pl.multiple_of(8 * j, 8)
        r0, rn, rs, ro = pl.ds(s, 8), pl.ds(s + 1, 8), pl.ds(s - 1, 8), pl.ds(t, 8)
        cols = slice(c * LANES, (c + 1) * LANES)
        ga = (0.5 * time_step) * inverse(q[fa, c, r0, :])
        gb = (0.5 * time_step) * inverse(q[fb, c, r0, :])
        rot = time_step * cor[c, ro, :]
        for l in range(levels):
            ce, cw = cf[l, c, r0, :], cf[levels + l, c, r0, :]
            cn, cs = cf[2 * levels + l, c, r0, :], cf[3 * levels + l, c, r0, :]
            wet = la[l, c, ro, :].astype(jnp.float32)

            def drag(v):
                f = v * levels + l
                x = lap[f, c, r0, :]
                xe, xw = to_e(x, lap[f, cp, r0, :]), to_w(x, lap[f, cm, r0, :])
                xn, xs = lap[f, c, rn, :], lap[f, c, rs, :]
                return ce * (xe - x) + cw * (xw - x) + cn * (xn - x) + cs * (xs - x)

            for i in range(2):
                ob[i * levels + l, ro, cols] = wet * (base[i * levels + l, c, r0, :] - drag(i))
            p = pres[l, c, r0, :]
            ge = (to_e(p, pres[l, cp, r0, :]) - to_w(p, pres[l, cm, r0, :])) * ga
            gn = (pres[l, c, rn, :] - pres[l, c, rs, :]) * gb
            u, v = q[2 * levels + l, c, r0, :], q[3 * levels + l, c, r0, :]
            ob[2 * levels + l, ro, cols] = wet * (u + (rot * v - ge) - drag(2))
            ob[3 * levels + l, ro, cols] = wet * (v - (rot * u + gn) - drag(3))

    outs = (temp_out, salt_out, uvel_out, vvel_out)

    def row_b(j):
        for c in range(nc):
            pass_b(j, c)

    stores = []
    size = rows // PARTS
    for part in range(PARTS):
        lo = part * size
        loop(size // 8, lambda j: row_b(lo // 8 + j))
        for i, dst in enumerate(outs):
            copy = pltpu.make_async_copy(
                ob.at[i * levels:(i + 1) * levels, lo:lo + size],
                dst.at[:, lo:lo + size],
                out_sem.at[part, i],
            )
            copy.start()
            stores.append(copy)
    for copy in stores:
        copy.wait()


def shards(n_lat, n_lon, *args):
    levels, rows, width = args[0].shape
    nc, nb, nf = width // LANES, rows // 8, 5 * levels + 2
    tall = rows + 2 * PAD
    row_slots = -(-2 * nf // 8) * 8
    f32 = jnp.float32

    def plane(count):
        return pltpu.VMEM((count, nc + 1, tall, LANES), f32)

    dma = pltpu.SemaphoreType.DMA
    held = pl.BlockSpec(memory_space=pltpu.VMEM)
    far = pl.BlockSpec(memory_space=pl.ANY)
    args = [pltpu.with_memory_space_constraint(x, pltpu.HBM) for x in args]
    middle = pl.pallas_call(
        functools.partial(first_kernel, n_lat, n_lon),
        out_shape=(
            plane(nf),
            pltpu.VMEM((levels, nc, rows, LANES), jnp.int32),
            pltpu.VMEM((nc, rows, LANES), f32),
            plane(4 * levels),
            plane(4 * levels),
            plane(levels),
            plane(2 * levels),
        ),
        in_specs=[far] * 9,
        out_specs=(held,) * 7,
        scratch_shapes=[
            pltpu.VMEM((levels, nc, rows, LANES), f32),
            pltpu.VMEM((2, nf, 8, width), f32),
            pltpu.VMEM((2, levels, 8, width), jnp.int32),
            pltpu.VMEM((2, nc, row_slots, LANES), f32),
            pltpu.VMEM((2, nc, row_slots, LANES), f32),
            pltpu.VMEM((2, nb, 8, LANES), f32),
            pltpu.VMEM((2, 8, LANES), f32),
            pltpu.VMEM((2, nb + 2, 8, LANES), f32),
            dma((16,)),
            dma((9 * nc,)),
            dma((2,)),
            dma((2,)),
            dma((2,)),
            dma((2, 3)),
            dma((4,)),
        ],
        compiler_params=pltpu.CompilerParams(
            collective_id=0, has_side_effects=True, vmem_limit_bytes=LIMIT * 1024 * 1024
        ),
    )(*args)
    return pl.pallas_call(
        second_kernel,
        out_shape=tuple(jax.ShapeDtypeStruct((levels, rows, width), f32) for _ in range(4)),
        in_specs=[held] * 7,
        out_specs=(far,) * 4,
        scratch_shapes=[
            pltpu.VMEM((4 * levels, rows, width), f32),
            dma((PARTS, 4)),
        ],
        compiler_params=pltpu.CompilerParams(vmem_limit_bytes=LIMIT * 1024 * 1024),
    )(*middle)


def solution(mesh):
    grid, line = P(None, "lat", "lon"), P("lat", "lon")
    body = functools.partial(shards, mesh.shape["lat"], mesh.shape["lon"])
    return jax.shard_map(
        body, mesh=mesh, in_specs=(grid,) * 6 + (line,) * 3, out_specs=(grid,) * 4, check_vma=False
    )
```

```python
import functools

import jax
import jax.numpy as jnp
from jax import lax
from jax.experimental import pallas as pl
from jax.experimental.pallas import tpu as pltpu
from jax.sharding import PartitionSpec as P

time_step = 0.2
biharm_coef = 0.02
alpha_temp = 0.2
beta_salt = 0.8
thin_floor = 0.25

LANES = 128
LIMIT = 32
PAD = 8


def inverse(x):
    return pl.reciprocal(x, approx=True)


def loop(count, body):
    lax.fori_loop(0, count, lambda i, carry: (body(i), carry)[1], 0)


def edge_lanes():
    lane = lax.broadcasted_iota(jnp.int32, (8, LANES), 1)
    first, last = lane == 0, lane == LANES - 1

    def to_e(x, beside):
        return pltpu.roll(jnp.where(first, beside, x), LANES - 1, 1)

    def to_w(x, beside):
        return pltpu.roll(jnp.where(last, beside, x), 1, 1)

    return lane, to_e, to_w


def first_kernel(
    n_lat, n_lon,
    temp, salt, uvel, vvel, thick, land, east_width, north_width, coriolis,
    q, la, cor, lap, cf, pres, base,
    th, edge, row_pack, row_recv, col_pack, corner_pack, col_recv,
    whole_sem, edge_sem, in_sem, row_send, row_sem, col_send, col_sem, corner_send,
):
    levels, rows, width = temp.shape
    nc = width // LANES
    nb = rows // 8
    nf = 5 * levels + 2
    fa, fb = 5 * levels, 5 * levels + 1
    lat, lon = lax.axis_index("lat"), lax.axis_index("lon")
    top = lat == n_lat - 1
    south = lat > 0
    east_lon = lax.rem(lon + 1, n_lon)
    west_lon = lax.rem(lon + n_lon - 1, n_lon)
    lat_n = jnp.where(top, lat, lat + 1)
    lat_s = jnp.where(south, lat - 1, 0)
    north = (lat_n, jnp.where(top, n_lon - 1 - lon, lon))
    fold_e = lax.rem(2 * n_lon - 2 - lon, n_lon)
    fold_w = lax.rem(n_lon - lon, n_lon)
    north_e = (lat_n, jnp.where(top, fold_e, east_lon))
    north_w = (lat_n, jnp.where(top, fold_w, west_lon))
    e_self = jnp.logical_and(top, fold_e == lon)
    w_self = jnp.logical_and(top, fold_w == lon)
    e_far, w_far = jnp.logical_not(e_self), jnp.logical_not(w_self)
    east, west = (lat, east_lon), (lat, west_lon)

    barrier = pltpu.get_barrier_semaphore()

    def greet(where):
        pl.semaphore_signal(barrier, inc=1, device_id={"lat": where[0], "lon": where[1]}, device_id_type=pl.DeviceIdType.MESH)

    greet(east)
    greet(west)
    greet(north)

    @pl.when(e_far)
    def _():
        greet(north_e)

    @pl.when(w_far)
    def _():
        greet(north_w)

    @pl.when(south)
    def _():
        greet((lat_s, lon))
        greet((lat_s, east_lon))
        greet((lat_s, west_lon))

    def begin(src, dst, sem):
        copy = pltpu.make_async_copy(src, dst, sem)
        copy.start()
        return copy

    whole = [begin(land, la, whole_sem.at[0]), begin(thick, th, whole_sem.at[1])]
    loads = {}

    def begin_tile(c):
        cols = pl.ds(c * LANES, LANES)
        here = []
        for i, src in enumerate((temp, salt, uvel, vvel)):
            here.append(begin(
                src.at[:, :, cols], q.at[i * levels:(i + 1) * levels, c, PAD:PAD + rows],
                in_sem.at[c, i],
            ))
        for i, src in enumerate((east_width, north_width)):
            here.append(begin(src.at[:, cols], q.at[fa + i, c, PAD:PAD + rows], in_sem.at[c, 4 + i]))
        loads[c] = here

    begin_tile(0)
    begin_tile(nc - 1)
    edge_loads = []
    for side, lo in ((0, 0), (1, rows - 8)):
        for i, src in enumerate((temp, salt, uvel, vvel)):
            edge_loads.append(begin(
                src.at[:, lo:lo + 8], edge.at[side, i * levels:(i + 1) * levels], edge_sem.at[side, i]
            ))
        for i, src in enumerate((east_width, north_width)):
            edge_loads.append(begin(src.at[lo:lo + 8], edge.at[side, fa + i], edge_sem.at[side, 4 + i]))
    for c in range(1, nc - 1):
        begin_tile(c)
    late = begin(coriolis, cor, whole_sem.at[2])

    lane, to_e, to_w = edge_lanes()
    sub = lax.broadcasted_iota(jnp.int32, (8, LANES), 0)

    def finish_load(c):
        for copy in loads[c]:
            copy.wait()
        for l in range(levels):
            cols = slice(c * LANES, (c + 1) * LANES)
            q[4 * levels + l, c, PAD:PAD + rows, :] = la[l, :, cols].astype(jnp.float32) * th[l, :, cols]

    for copy in whole:
        copy.wait()

    finish_load(0)
    finish_load(nc - 1)
    lane_r = lax.broadcasted_iota(jnp.int32, (rows, LANES), 1)
    head = jnp.zeros((rows, LANES), jnp.float32)
    tail = jnp.zeros((rows, LANES), jnp.float32)
    for f in range(nf):
        mine = lane_r // 2 == f
        a0 = q[f, 0, PAD:PAD + rows, :]
        a1 = q[f, nc - 1, PAD:PAD + rows, :]
        head = jnp.where(mine, pltpu.roll(a0, 2 * f, 1) if f else a0, head)
        tail = jnp.where(mine, pltpu.roll(a1, 2 * f + 2, 1), tail)
    col_pack[0] = head.reshape(nb, 8, LANES)
    col_pack[1] = tail.reshape(nb, 8, LANES)
    sign_lane = jnp.where(
        jnp.logical_and(lane >= 4 * levels, lane < 8 * levels), -1.0, 1.0
    ).astype(jnp.float32)
    for side, block in ((0, head), (1, tail)):
        x = block[rows - 8:rows, :]
        y = jnp.where(lane % 2 == 0, pltpu.roll(x, LANES - 1, 1), pltpu.roll(x, 1, 1)) * sign_lane
        y = jnp.where(sub == 0, pltpu.roll(y, 2, 0), pltpu.roll(y, 4, 0))
        corner_pack[side] = jnp.where(top, y, x)

    partners = 3 + e_far.astype(jnp.int32) + w_far.astype(jnp.int32) + 3 * south.astype(jnp.int32)
    pl.semaphore_wait(barrier, partners)

    def send(src, dst, s_sem, r_sem, where):
        return pltpu.make_async_remote_copy(
            src_ref=src, dst_ref=dst, send_sem=s_sem, recv_sem=r_sem,
            device_id={"lat": where[0], "lon": where[1]}, device_id_type=pl.DeviceIdType.MESH,
        )

    to_east = send(col_pack.at[1], col_recv.at[1, 1:nb + 1], col_send.at[1], col_sem.at[1, 1], east)
    to_west = send(col_pack.at[0], col_recv.at[0, 1:nb + 1], col_send.at[0], col_sem.at[0, 1], west)
    e_side = jnp.where(top, 0, 1)
    w_side = jnp.where(top, 1, 0)
    blk = jnp.where(top, nb + 1, 0)
    which = jnp.where(top, 2, 0)
    to_ne = send(corner_pack.at[1], col_recv.at[e_side, blk], corner_send.at[0], col_sem.at[e_side, which], north_e)
    to_nw = send(corner_pack.at[0], col_recv.at[w_side, blk], corner_send.at[1], col_sem.at[w_side, which], north_w)
    to_se = send(col_pack.at[1, 0], col_recv.at[1, nb + 1], corner_send.at[2], col_sem.at[1, 2], (lat_s, east_lon))
    to_sw = send(col_pack.at[0, 0], col_recv.at[0, nb + 1], corner_send.at[3], col_sem.at[0, 2], (lat_s, west_lon))
    to_east.start()
    to_west.start()

    @pl.when(south)
    def _():
        to_se.start()
        to_sw.start()

    @pl.when(e_far)
    def _():
        to_ne.start()

    @pl.when(w_far)
    def _():
        to_nw.start()

    for copy in edge_loads:
        copy.wait()
    flip = jnp.where(top, -1.0, 1.0).astype(jnp.float32)
    for side in range(2):
        for l in range(levels):
            f = 4 * levels + l
            lo = (rows - 8) * side
            edge[side, f] = la[l, lo:lo + 8].astype(jnp.float32) * th[l, lo:lo + 8]
    for f in range(nf):
        for c in range(nc):
            cols = slice(c * LANES, (c + 1) * LANES)
            row_pack[0, c, 2 * f:2 * f + 2, :] = edge[0, f, 0:2, cols]
            near = edge[1, f, 6:7, cols]
            far = jnp.where(top, edge[1, f, 5:6, cols], edge[1, f, 7:8, cols])
            if 2 * levels <= f < 4 * levels:
                near, far = near * flip, far * flip
            row_pack[1, c, 2 * f:2 * f + 1, :] = near
            row_pack[1, c, 2 * f + 1:2 * f + 2, :] = far

    @pl.when(top)
    def _():
        i0 = lax.broadcasted_iota(jnp.int32, (LANES, LANES), 0)
        i1 = lax.broadcasted_iota(jnp.int32, (LANES, LANES), 1)
        mirror = (i0 + i1 == LANES - 1).astype(jnp.float32)
        turned = [
            jnp.dot(row_pack[1, c, 0:2 * nf, :], mirror, precision=lax.Precision.HIGHEST,
                    preferred_element_type=jnp.float32)
            for c in range(nc)
        ]
        for c in range(nc):
            row_pack[1, nc - 1 - c, 0:2 * nf, :] = turned[c]

    slot = jnp.where(top, 1, 0)
    to_north = send(row_pack.at[1], row_recv.at[slot], row_send.at[1], row_sem.at[slot], north)
    to_south = send(row_pack.at[0], row_recv.at[1], row_send.at[0], row_sem.at[1], (lat_s, lon))
    to_north.start()

    @pl.when(south)
    def _():
        to_south.start()

    for c in range(1, nc - 1):
        finish_load(c)
    ring = nc + 1

    def pass_a(s, c):
        cp, cm = (c + 1) % ring, (c - 1) % ring
        r0, rn, rs = pl.ds(s, 8), pl.ds(s + 1, 8), pl.ds(s - 1, 8)

        def five(f):
            x = q[f, c, r0, :]
            return (x, to_e(x, q[f, cp, r0, :]), to_w(x, q[f, cm, r0, :]), q[f, c, rn, :], q[f, c, rs, :])

        a, ae, aw, an, as_ = five(fa)
        b, be, bw, bn, bs = five(fb)
        area = a * b
        root = biharm_coef ** 0.5
        we, ww, wn, ws = b + be, b + bw, a + an, a + as_
        re, rw = (root * we) * inverse(a + ae), (root * ww) * inverse(a + aw)
        rn_, rs_ = (root * wn) * inverse(b + bn), (root * ws) * inverse(b + bs)
        k = time_step / 8.0
        we, ww, wn, ws = we * k, ww * k, wn * k, ws * k
        over = jnp.zeros_like(a)
        for l in range(levels):
            d, de, dw, dn, ds_ = five(4 * levels + l)
            inv = inverse(area * jnp.maximum(d, thin_floor))
            me = jnp.minimum(d, de) * inv
            mw = jnp.minimum(d, dw) * inv
            mn = jnp.minimum(d, dn) * inv
            ms = jnp.minimum(d, ds_) * inv
            ce, cw, cn, cs = me * re, mw * rw, mn * rn_, ms * rs_
            if c < nc:
                cf[l, c, r0, :] = ce
                cf[levels + l, c, r0, :] = cw
                cf[2 * levels + l, c, r0, :] = cn
                cf[3 * levels + l, c, r0, :] = cs

            def laplace(v, x, xe, xw, xn, xs):
                lap[v * levels + l, c, r0, :] = (
                    ce * (xe - x) + cw * (xw - x) + cn * (xn - x) + cs * (xs - x)
                )

            u = five(2 * levels + l)
            laplace(2, *u)
            te = me * we * (u[0] + u[1])
            tw = mw * ww * (u[0] + u[2])
            v = five(3 * levels + l)
            laplace(3, *v)
            tn = mn * wn * (v[0] + v[3])
            ts = ms * ws * (v[0] + v[4])
            tracer = []
            for i in range(2):
                x, xe, xw, xn, xs = five(i * levels + l)
                laplace(i, x, xe, xw, xn, xs)
                if c < nc:
                    advect = te * (x + xe) - tw * (x + xw) + tn * (x + xn) - ts * (x + xs)
                    base[i * levels + l, c, r0, :] = x - advect
                tracer.append(x)
            buoyancy = (beta_salt * tracer[1] - alpha_temp * tracer[0]) * d
            pres[l, c, r0, :] = over + 0.5 * buoyancy
            over = over + buoyancy

    def row_a(s, tiles):
        for c in tiles:
            pass_a(s, c)

    def unpack_cols(block):
        s = pl.multiple_of(8 * block, 8)
        e, w = col_recv[0, block], col_recv[1, block]
        for f in range(nf):
            x = pltpu.roll(e, LANES - 2 * f, 1) if f else e
            q[f, nc, pl.ds(s, 8), :] = jnp.where(lane < 64, x, pltpu.roll(w, LANES - 2 - 2 * f, 1))

    loop(nb - 1, lambda k: row_a(PAD - 1 + 8 * (1 + k), range(1, nc - 1)))
    to_east.wait_recv()
    to_west.wait_recv()
    loop(nb, lambda i: unpack_cols(i + 1))
    loop(nb - 1, lambda k: row_a(PAD - 1 + 8 * (1 + k), (nc - 1, nc, 0)))

    @pl.when(south)
    def _():
        send(row_pack.at[1], row_recv.at[0], row_send.at[1], row_sem.at[0], north).wait_recv()
        send(corner_pack.at[1], col_recv.at[1, 0], corner_send.at[0], col_sem.at[1, 0], east).wait_recv()
        send(corner_pack.at[0], col_recv.at[0, 0], corner_send.at[1], col_sem.at[0, 0], west).wait_recv()
        for f in range(nf):
            q[f, 0:nc, PAD - 2:PAD, :] = row_recv[0, :, 2 * f:2 * f + 2, :]
        unpack_cols(0)

    @pl.when(jnp.logical_not(south))
    def _():
        for f in range(nf):
            q[f, :, 0:PAD, :] = jnp.full((ring, PAD, LANES), 1.0 if f >= fa else 0.0, jnp.float32)

    send(row_pack.at[0], row_recv.at[1], row_send.at[0], row_sem.at[1], north).wait_recv()

    @pl.when(e_far)
    def _():
        send(corner_pack.at[1], col_recv.at[0, nb + 1], corner_send.at[0], col_sem.at[0, 2], east).wait_recv()

    @pl.when(e_self)
    def _():
        col_recv[0, nb + 1] = corner_pack[1]

    @pl.when(w_far)
    def _():
        send(corner_pack.at[0], col_recv.at[1, nb + 1], corner_send.at[1], col_sem.at[1, 2], west).wait_recv()

    @pl.when(w_self)
    def _():
        col_recv[1, nb + 1] = corner_pack[0]

    for f in range(nf):
        q[f, 0:nc, PAD + rows:PAD + rows + 2, :] = row_recv[1, :, 2 * f:2 * f + 2, :]
    unpack_cols(nb + 1)

    loop(2, lambda i: row_a(PAD - 1 + (rows - 6) * i, range(ring)))

    late.wait()
    to_east.wait_send()
    to_west.wait_send()
    to_north.wait_send()

    @pl.when(south)
    def _():
        to_south.wait_send()
        to_se.wait_send()
        to_sw.wait_send()

    @pl.when(e_far)
    def _():
        to_ne.wait_send()

    @pl.when(w_far)
    def _():
        to_nw.wait_send()


def second_kernel(
    q, la, cor, lap, cf, pres, base, temp_out, salt_out, uvel_out, vvel_out,
    ob, out_sem,
):
    levels, rows, width = temp_out.shape
    nc, nb = width // LANES, rows // 8
    fa, fb = 5 * levels, 5 * levels + 1
    ring = nc + 1
    lane, to_e, to_w = edge_lanes()

    def pass_b(j, c):
        cp, cm = (c + 1) % ring, (c - 1) % ring
        s = pl.multiple_of(PAD + 8 * j, 8)
        t = pl.multiple_of(8 * j, 8)
        r0, rn, rs, ro = pl.ds(s, 8), pl.ds(s + 1, 8), pl.ds(s - 1, 8), pl.ds(t, 8)
        cols = slice(c * LANES, (c + 1) * LANES)
        ga = (0.5 * time_step) * inverse(q[fa, c, r0, :])
        gb = (0.5 * time_step) * inverse(q[fb, c, r0, :])
        rot = time_step * cor[ro, cols]
        for l in range(levels):
            ce, cw = cf[l, c, r0, :], cf[levels + l, c, r0, :]
            cn, cs = cf[2 * levels + l, c, r0, :], cf[3 * levels + l, c, r0, :]
            wet = la[l, ro, cols].astype(jnp.float32)

            def drag(v):
                f = v * levels + l
                x = lap[f, c, r0, :]
                xe, xw = to_e(x, lap[f, cp, r0, :]), to_w(x, lap[f, cm, r0, :])
                xn, xs = lap[f, c, rn, :], lap[f, c, rs, :]
                return ce * (xe - x) + cw * (xw - x) + cn * (xn - x) + cs * (xs - x)

            for i in range(2):
                ob[i * levels + l, ro, cols] = wet * (base[i * levels + l, c, r0, :] - drag(i))
            p = pres[l, c, r0, :]
            ge = (to_e(p, pres[l, cp, r0, :]) - to_w(p, pres[l, cm, r0, :])) * ga
            gn = (pres[l, c, rn, :] - pres[l, c, rs, :]) * gb
            u, v = q[2 * levels + l, c, r0, :], q[3 * levels + l, c, r0, :]
            ob[2 * levels + l, ro, cols] = wet * (u + (rot * v - ge) - drag(2))
            ob[3 * levels + l, ro, cols] = wet * (v - (rot * u + gn) - drag(3))

    outs = (temp_out, salt_out, uvel_out, vvel_out)

    def store(j):
        t = pl.multiple_of(8 * j, 8)
        return [
            pltpu.make_async_copy(
                ob.at[i * levels:(i + 1) * levels, pl.ds(t, 8)], dst.at[:, pl.ds(t, 8)], out_sem.at[j, i]
            )
            for i, dst in enumerate(outs)
        ]

    def row_b(j):
        for c in range(nc):
            pass_b(j, c)
        for copy in store(j):
            copy.start()

    def settle(j):
        for copy in store(j):
            copy.wait()

    loop(nb, row_b)
    loop(nb, settle)


def shards(n_lat, n_lon, *args):
    levels, rows, width = args[0].shape
    nc, nb, nf = width // LANES, rows // 8, 5 * levels + 2
    tall = rows + 2 * PAD
    row_slots = -(-2 * nf // 8) * 8
    f32 = jnp.float32

    def plane(count):
        return pltpu.VMEM((count, nc + 1, tall, LANES), f32)

    dma = pltpu.SemaphoreType.DMA
    held = pl.BlockSpec(memory_space=pltpu.VMEM)
    far = pl.BlockSpec(memory_space=pl.ANY)
    args = [pltpu.with_memory_space_constraint(x, pltpu.HBM) for x in args]
    middle = pl.pallas_call(
        functools.partial(first_kernel, n_lat, n_lon),
        out_shape=(
            plane(nf),
            pltpu.VMEM((levels, rows, width), jnp.int32),
            pltpu.VMEM((rows, width), f32),
            plane(4 * levels),
            plane(4 * levels),
            plane(levels),
            plane(2 * levels),
        ),
        in_specs=[far] * 9,
        out_specs=(held,) * 7,
        scratch_shapes=[
            pltpu.VMEM((levels, rows, width), f32),
            pltpu.VMEM((2, nf, 8, width), f32),
            pltpu.VMEM((2, nc, row_slots, LANES), f32),
            pltpu.VMEM((2, nc, row_slots, LANES), f32),
            pltpu.VMEM((2, nb, 8, LANES), f32),
            pltpu.VMEM((2, 8, LANES), f32),
            pltpu.VMEM((2, nb + 2, 8, LANES), f32),
            dma((3,)),
            dma((2, 6)),
            dma((nc, 6)),
            dma((2,)),
            dma((2,)),
            dma((2,)),
            dma((2, 3)),
            dma((4,)),
        ],
        compiler_params=pltpu.CompilerParams(
            collective_id=0, has_side_effects=True, vmem_limit_bytes=LIMIT * 1024 * 1024
        ),
    )(*args)
    return pl.pallas_call(
        second_kernel,
        out_shape=tuple(jax.ShapeDtypeStruct((levels, rows, width), f32) for _ in range(4)),
        in_specs=[held] * 7,
        out_specs=(far,) * 4,
        scratch_shapes=[
            pltpu.VMEM((4 * levels, rows, width), f32),
            dma((nb, 4)),
        ],
        compiler_params=pltpu.CompilerParams(vmem_limit_bytes=LIMIT * 1024 * 1024),
    )(*middle)


def solution(mesh):
    grid, line = P(None, "lat", "lon"), P("lat", "lon")
    body = functools.partial(shards, mesh.shape["lat"], mesh.shape["lon"])
    return jax.shard_map(
        body, mesh=mesh, in_specs=(grid,) * 6 + (line,) * 3, out_specs=(grid,) * 4, check_vma=False
    )
```

```python
import functools

import jax
import jax.numpy as jnp
from jax import lax
from jax.experimental import pallas as pl
from jax.experimental.pallas import tpu as pltpu
from jax.sharding import PartitionSpec as P

time_step = 0.2
biharm_coef = 0.02
alpha_temp = 0.2
beta_salt = 0.8
thin_floor = 0.25

LANES = 128
LIMIT = 32
PAD = 8


def inverse(x):
    return pl.reciprocal(x, approx=True)


def loop(count, body):
    lax.fori_loop(0, count, lambda i, carry: (body(i), carry)[1], 0)


def edge_lanes():
    lane = lax.broadcasted_iota(jnp.int32, (8, LANES), 1)
    first, last = lane == 0, lane == LANES - 1

    def to_e(x, beside):
        return pltpu.roll(jnp.where(first, beside, x), LANES - 1, 1)

    def to_w(x, beside):
        return pltpu.roll(jnp.where(last, beside, x), 1, 1)

    return lane, to_e, to_w


def first_kernel(
    n_lat, n_lon,
    temp, salt, uvel, vvel, thick, land, east_width, north_width, coriolis,
    q, la, cor, lap, cf, pres, base,
    th, edge, row_pack, row_recv, col_pack, corner_pack, col_recv,
    whole_sem, edge_sem, in_sem, row_send, row_sem, col_send, col_sem, corner_send,
):
    levels, rows, width = temp.shape
    nc = width // LANES
    nb = rows // 8
    nf = 5 * levels + 2
    fa, fb = 5 * levels, 5 * levels + 1
    lat, lon = lax.axis_index("lat"), lax.axis_index("lon")
    top = lat == n_lat - 1
    south = lat > 0
    east_lon = lax.rem(lon + 1, n_lon)
    west_lon = lax.rem(lon + n_lon - 1, n_lon)
    lat_n = jnp.where(top, lat, lat + 1)
    lat_s = jnp.where(south, lat - 1, 0)
    north = (lat_n, jnp.where(top, n_lon - 1 - lon, lon))
    fold_e = lax.rem(2 * n_lon - 2 - lon, n_lon)
    fold_w = lax.rem(n_lon - lon, n_lon)
    north_e = (lat_n, jnp.where(top, fold_e, east_lon))
    north_w = (lat_n, jnp.where(top, fold_w, west_lon))
    e_self = jnp.logical_and(top, fold_e == lon)
    w_self = jnp.logical_and(top, fold_w == lon)
    e_far, w_far = jnp.logical_not(e_self), jnp.logical_not(w_self)
    east, west = (lat, east_lon), (lat, west_lon)

    barrier = pltpu.get_barrier_semaphore()

    def greet(where):
        pl.semaphore_signal(barrier, inc=1, device_id={"lat": where[0], "lon": where[1]}, device_id_type=pl.DeviceIdType.MESH)

    greet(east)
    greet(west)
    greet(north)

    @pl.when(e_far)
    def _():
        greet(north_e)

    @pl.when(w_far)
    def _():
        greet(north_w)

    @pl.when(south)
    def _():
        greet((lat_s, lon))
        greet((lat_s, east_lon))
        greet((lat_s, west_lon))

    def begin(src, dst, sem):
        copy = pltpu.make_async_copy(src, dst, sem)
        copy.start()
        return copy

    whole = [begin(land, la, whole_sem.at[0]), begin(thick, th, whole_sem.at[1])]
    loads = {}

    def begin_tile(c):
        cols = pl.ds(c * LANES, LANES)
        here = []
        for i, src in enumerate((temp, salt, uvel, vvel)):
            here.append(begin(
                src.at[:, :, cols], q.at[i * levels:(i + 1) * levels, c, PAD:PAD + rows],
                in_sem.at[c, i],
            ))
        for i, src in enumerate((east_width, north_width)):
            here.append(begin(src.at[:, cols], q.at[fa + i, c, PAD:PAD + rows], in_sem.at[c, 4 + i]))
        loads[c] = here

    begin_tile(0)
    begin_tile(nc - 1)
    edge_loads = []
    for side, lo in ((0, 0), (1, rows - 8)):
        for i, src in enumerate((temp, salt, uvel, vvel)):
            edge_loads.append(begin(
                src.at[:, lo:lo + 8], edge.at[side, i * levels:(i + 1) * levels], edge_sem.at[side, i]
            ))
        for i, src in enumerate((east_width, north_width)):
            edge_loads.append(begin(src.at[lo:lo + 8], edge.at[side, fa + i], edge_sem.at[side, 4 + i]))
    for c in range(1, nc - 1):
        begin_tile(c)
    late = begin(coriolis, cor, whole_sem.at[2])

    lane, to_e, to_w = edge_lanes()
    sub = lax.broadcasted_iota(jnp.int32, (8, LANES), 0)

    def finish_load(c):
        for copy in loads[c]:
            copy.wait()
        for l in range(levels):
            cols = slice(c * LANES, (c + 1) * LANES)
            q[4 * levels + l, c, PAD:PAD + rows, :] = la[l, :, cols].astype(jnp.float32) * th[l, :, cols]

    for copy in whole:
        copy.wait()

    finish_load(0)
    finish_load(nc - 1)
    own = [jnp.logical_and(lane >= 4 * f, lane < 4 * f + 4) for f in range(nf)]

    def pack_cols(k):
        r = pl.ds(pl.multiple_of(PAD + 8 * k, 8), 8)
        block = jnp.zeros((8, LANES), jnp.float32)
        for f in range(nf):
            ends = jnp.where(lane < LANES // 2, q[f, 0, r, :], q[f, nc - 1, r, :])
            block = jnp.where(own[f], pltpu.roll(ends, 4 * f + 2, 1), block)
        col_pack[k] = block

    loop(nb, pack_cols)
    sign_lane = jnp.where(
        jnp.logical_and(lane >= 8 * levels, lane < 16 * levels), -1.0, 1.0
    ).astype(jnp.float32)
    x = col_pack[nb - 1]
    place = lane % 4
    y = jnp.where(
        place < 2,
        jnp.where(place == 0, pltpu.roll(x, LANES - 3, 1), pltpu.roll(x, LANES - 1, 1)),
        jnp.where(place == 2, pltpu.roll(x, 1, 1), pltpu.roll(x, 3, 1)),
    ) * sign_lane
    y = jnp.where(sub == 0, pltpu.roll(y, 2, 0), pltpu.roll(y, 4, 0))
    corner_pack[...] = jnp.where(top, y, x)

    partners = 3 + e_far.astype(jnp.int32) + w_far.astype(jnp.int32) + 3 * south.astype(jnp.int32)
    pl.semaphore_wait(barrier, partners)

    def send(src, dst, s_sem, r_sem, where):
        return pltpu.make_async_remote_copy(
            src_ref=src, dst_ref=dst, send_sem=s_sem, recv_sem=r_sem,
            device_id={"lat": where[0], "lon": where[1]}, device_id_type=pl.DeviceIdType.MESH,
        )

    to_east = send(col_pack, col_recv.at[1, 1:nb + 1], col_send.at[1], col_sem.at[1, 1], east)
    to_west = send(col_pack, col_recv.at[0, 1:nb + 1], col_send.at[0], col_sem.at[0, 1], west)
    e_side = jnp.where(top, 0, 1)
    w_side = jnp.where(top, 1, 0)
    blk = jnp.where(top, nb + 1, 0)
    which = jnp.where(top, 2, 0)
    to_ne = send(corner_pack, col_recv.at[e_side, blk], corner_send.at[0], col_sem.at[e_side, which], north_e)
    to_nw = send(corner_pack, col_recv.at[w_side, blk], corner_send.at[1], col_sem.at[w_side, which], north_w)
    to_se = send(col_pack.at[0], col_recv.at[1, nb + 1], corner_send.at[2], col_sem.at[1, 2], (lat_s, east_lon))
    to_sw = send(col_pack.at[0], col_recv.at[0, nb + 1], corner_send.at[3], col_sem.at[0, 2], (lat_s, west_lon))
    to_east.start()
    to_west.start()

    @pl.when(south)
    def _():
        to_se.start()
        to_sw.start()

    @pl.when(e_far)
    def _():
        to_ne.start()

    @pl.when(w_far)
    def _():
        to_nw.start()

    for copy in edge_loads:
        copy.wait()
    flip = jnp.where(top, -1.0, 1.0).astype(jnp.float32)
    for side in range(2):
        for l in range(levels):
            f = 4 * levels + l
            lo = (rows - 8) * side
            edge[side, f] = la[l, lo:lo + 8].astype(jnp.float32) * th[l, lo:lo + 8]
    for f in range(nf):
        for c in range(nc):
            cols = slice(c * LANES, (c + 1) * LANES)
            row_pack[0, c, 2 * f:2 * f + 2, :] = edge[0, f, 0:2, cols]
            near = edge[1, f, 6:7, cols]
            far = jnp.where(top, edge[1, f, 5:6, cols], edge[1, f, 7:8, cols])
            if 2 * levels <= f < 4 * levels:
                near, far = near * flip, far * flip
            row_pack[1, c, 2 * f:2 * f + 1, :] = near
            row_pack[1, c, 2 * f + 1:2 * f + 2, :] = far

    @pl.when(top)
    def _():
        i0 = lax.broadcasted_iota(jnp.int32, (LANES, LANES), 0)
        i1 = lax.broadcasted_iota(jnp.int32, (LANES, LANES), 1)
        mirror = (i0 + i1 == LANES - 1).astype(jnp.float32)
        turned = [
            jnp.dot(row_pack[1, c, 0:2 * nf, :], mirror, precision=lax.Precision.HIGHEST,
                    preferred_element_type=jnp.float32)
            for c in range(nc)
        ]
        for c in range(nc):
            row_pack[1, nc - 1 - c, 0:2 * nf, :] = turned[c]

    slot = jnp.where(top, 1, 0)
    to_north = send(row_pack.at[1], row_recv.at[slot], row_send.at[1], row_sem.at[slot], north)
    to_south = send(row_pack.at[0], row_recv.at[1], row_send.at[0], row_sem.at[1], (lat_s, lon))
    to_north.start()

    @pl.when(south)
    def _():
        to_south.start()

    for c in range(1, nc - 1):
        finish_load(c)
    ring = nc + 1

    def pass_a(s, c):
        cp, cm = (c + 1) % ring, (c - 1) % ring
        r0, rn, rs = pl.ds(s, 8), pl.ds(s + 1, 8), pl.ds(s - 1, 8)

        def five(f):
            x = q[f, c, r0, :]
            return (x, to_e(x, q[f, cp, r0, :]), to_w(x, q[f, cm, r0, :]), q[f, c, rn, :], q[f, c, rs, :])

        a, ae, aw, an, as_ = five(fa)
        b, be, bw, bn, bs = five(fb)
        area = a * b
        root = biharm_coef ** 0.5
        we, ww, wn, ws = b + be, b + bw, a + an, a + as_
        re, rw = (root * we) * inverse(a + ae), (root * ww) * inverse(a + aw)
        rn_, rs_ = (root * wn) * inverse(b + bn), (root * ws) * inverse(b + bs)
        k = time_step / 8.0
        we, ww, wn, ws = we * k, ww * k, wn * k, ws * k
        over = jnp.zeros_like(a)
        for l in range(levels):
            d, de, dw, dn, ds_ = five(4 * levels + l)
            inv = inverse(area * jnp.maximum(d, thin_floor))
            me = jnp.minimum(d, de) * inv
            mw = jnp.minimum(d, dw) * inv
            mn = jnp.minimum(d, dn) * inv
            ms = jnp.minimum(d, ds_) * inv
            ce, cw, cn, cs = me * re, mw * rw, mn * rn_, ms * rs_
            if c < nc:
                cf[l, c, r0, :] = ce
                cf[levels + l, c, r0, :] = cw
                cf[2 * levels + l, c, r0, :] = cn
                cf[3 * levels + l, c, r0, :] = cs

            def laplace(v, x, xe, xw, xn, xs):
                lap[v * levels + l, c, r0, :] = (
                    ce * (xe - x) + cw * (xw - x) + cn * (xn - x) + cs * (xs - x)
                )

            u = five(2 * levels + l)
            laplace(2, *u)
            te = me * we * (u[0] + u[1])
            tw = mw * ww * (u[0] + u[2])
            v = five(3 * levels + l)
            laplace(3, *v)
            tn = mn * wn * (v[0] + v[3])
            ts = ms * ws * (v[0] + v[4])
            tracer = []
            for i in range(2):
                x, xe, xw, xn, xs = five(i * levels + l)
                laplace(i, x, xe, xw, xn, xs)
                if c < nc:
                    advect = te * (x + xe) - tw * (x + xw) + tn * (x + xn) - ts * (x + xs)
                    base[i * levels + l, c, r0, :] = x - advect
                tracer.append(x)
            buoyancy = (beta_salt * tracer[1] - alpha_temp * tracer[0]) * d
            pres[l, c, r0, :] = over + 0.5 * buoyancy
            over = over + buoyancy

    def row_a(s, tiles):
        for c in tiles:
            pass_a(s, c)

    def unpack_cols(block):
        s = pl.multiple_of(8 * block, 8)
        both = jnp.where(lane % 4 < 2, col_recv[1, block], col_recv[0, block])
        for f in range(nf):
            q[f, nc, pl.ds(s, 8), :] = pltpu.roll(both, LANES - 2 - 4 * f, 1)

    loop(nb - 1, lambda k: row_a(PAD - 1 + 8 * (1 + k), range(1, nc - 1)))
    to_east.wait_recv()
    to_west.wait_recv()
    loop(nb, lambda i: unpack_cols(i + 1))
    loop(nb - 1, lambda k: row_a(PAD - 1 + 8 * (1 + k), (nc - 1, nc, 0)))

    @pl.when(south)
    def _():
        send(row_pack.at[1], row_recv.at[0], row_send.at[1], row_sem.at[0], north).wait_recv()
        send(corner_pack, col_recv.at[1, 0], corner_send.at[0], col_sem.at[1, 0], east).wait_recv()
        send(corner_pack, col_recv.at[0, 0], corner_send.at[1], col_sem.at[0, 0], west).wait_recv()
        for f in range(nf):
            q[f, 0:nc, PAD - 2:PAD, :] = row_recv[0, :, 2 * f:2 * f + 2, :]
        unpack_cols(0)

    @pl.when(jnp.logical_not(south))
    def _():
        for f in range(nf):
            q[f, :, 0:PAD, :] = jnp.full((ring, PAD, LANES), 1.0 if f >= fa else 0.0, jnp.float32)

    send(row_pack.at[0], row_recv.at[1], row_send.at[0], row_sem.at[1], north).wait_recv()

    @pl.when(e_far)
    def _():
        send(corner_pack, col_recv.at[0, nb + 1], corner_send.at[0], col_sem.at[0, 2], east).wait_recv()

    @pl.when(e_self)
    def _():
        col_recv[0, nb + 1] = corner_pack[...]

    @pl.when(w_far)
    def _():
        send(corner_pack, col_recv.at[1, nb + 1], corner_send.at[1], col_sem.at[1, 2], west).wait_recv()

    @pl.when(w_self)
    def _():
        col_recv[1, nb + 1] = corner_pack[...]

    for f in range(nf):
        q[f, 0:nc, PAD + rows:PAD + rows + 2, :] = row_recv[1, :, 2 * f:2 * f + 2, :]
    unpack_cols(nb + 1)

    loop(2, lambda i: row_a(PAD - 1 + (rows - 6) * i, range(ring)))

    late.wait()
    to_east.wait_send()
    to_west.wait_send()
    to_north.wait_send()

    @pl.when(south)
    def _():
        to_south.wait_send()
        to_se.wait_send()
        to_sw.wait_send()

    @pl.when(e_far)
    def _():
        to_ne.wait_send()

    @pl.when(w_far)
    def _():
        to_nw.wait_send()


def second_kernel(
    q, la, cor, lap, cf, pres, base, temp_out, salt_out, uvel_out, vvel_out,
    ob, out_sem,
):
    levels, rows, width = temp_out.shape
    nc, nb = width // LANES, rows // 8
    fa, fb = 5 * levels, 5 * levels + 1
    ring = nc + 1
    lane, to_e, to_w = edge_lanes()

    def pass_b(j, c):
        cp, cm = (c + 1) % ring, (c - 1) % ring
        s = pl.multiple_of(PAD + 8 * j, 8)
        t = pl.multiple_of(8 * j, 8)
        r0, rn, rs, ro = pl.ds(s, 8), pl.ds(s + 1, 8), pl.ds(s - 1, 8), pl.ds(t, 8)
        cols = slice(c * LANES, (c + 1) * LANES)
        ga = (0.5 * time_step) * inverse(q[fa, c, r0, :])
        gb = (0.5 * time_step) * inverse(q[fb, c, r0, :])
        rot = time_step * cor[ro, cols]
        for l in range(levels):
            ce, cw = cf[l, c, r0, :], cf[levels + l, c, r0, :]
            cn, cs = cf[2 * levels + l, c, r0, :], cf[3 * levels + l, c, r0, :]
            wet = la[l, ro, cols].astype(jnp.float32)

            def drag(v):
                f = v * levels + l
                x = lap[f, c, r0, :]
                xe, xw = to_e(x, lap[f, cp, r0, :]), to_w(x, lap[f, cm, r0, :])
                xn, xs = lap[f, c, rn, :], lap[f, c, rs, :]
                return ce * (xe - x) + cw * (xw - x) + cn * (xn - x) + cs * (xs - x)

            for i in range(2):
                ob[i * levels + l, ro, cols] = wet * (base[i * levels + l, c, r0, :] - drag(i))
            p = pres[l, c, r0, :]
            ge = (to_e(p, pres[l, cp, r0, :]) - to_w(p, pres[l, cm, r0, :])) * ga
            gn = (pres[l, c, rn, :] - pres[l, c, rs, :]) * gb
            u, v = q[2 * levels + l, c, r0, :], q[3 * levels + l, c, r0, :]
            ob[2 * levels + l, ro, cols] = wet * (u + (rot * v - ge) - drag(2))
            ob[3 * levels + l, ro, cols] = wet * (v - (rot * u + gn) - drag(3))

    outs = (temp_out, salt_out, uvel_out, vvel_out)

    def store(j):
        t = pl.multiple_of(8 * j, 8)
        return [
            pltpu.make_async_copy(
                ob.at[i * levels:(i + 1) * levels, pl.ds(t, 8)], dst.at[:, pl.ds(t, 8)], out_sem.at[j, i]
            )
            for i, dst in enumerate(outs)
        ]

    def row_b(j):
        for c in range(nc):
            pass_b(j, c)
        for copy in store(j):
            copy.start()

    def settle(j):
        for copy in store(j):
            copy.wait()

    loop(nb, row_b)
    loop(nb, settle)


def shards(n_lat, n_lon, *args):
    levels, rows, width = args[0].shape
    nc, nb, nf = width // LANES, rows // 8, 5 * levels + 2
    tall = rows + 2 * PAD
    row_slots = -(-2 * nf // 8) * 8
    f32 = jnp.float32

    def plane(count):
        return pltpu.VMEM((count, nc + 1, tall, LANES), f32)

    dma = pltpu.SemaphoreType.DMA
    held = pl.BlockSpec(memory_space=pltpu.VMEM)
    far = pl.BlockSpec(memory_space=pl.ANY)
    args = [pltpu.with_memory_space_constraint(x, pltpu.HBM) for x in args]
    middle = pl.pallas_call(
        functools.partial(first_kernel, n_lat, n_lon),
        out_shape=(
            plane(nf),
            pltpu.VMEM((levels, rows, width), jnp.int32),
            pltpu.VMEM((rows, width), f32),
            plane(4 * levels),
            plane(4 * levels),
            plane(levels),
            plane(2 * levels),
        ),
        in_specs=[far] * 9,
        out_specs=(held,) * 7,
        scratch_shapes=[
            pltpu.VMEM((levels, rows, width), f32),
            pltpu.VMEM((2, nf, 8, width), f32),
            pltpu.VMEM((2, nc, row_slots, LANES), f32),
            pltpu.VMEM((2, nc, row_slots, LANES), f32),
            pltpu.VMEM((nb, 8, LANES), f32),
            pltpu.VMEM((8, LANES), f32),
            pltpu.VMEM((2, nb + 2, 8, LANES), f32),
            dma((3,)),
            dma((2, 6)),
            dma((nc, 6)),
            dma((2,)),
            dma((2,)),
            dma((2,)),
            dma((2, 3)),
            dma((4,)),
        ],
        compiler_params=pltpu.CompilerParams(
            collective_id=0, has_side_effects=True, vmem_limit_bytes=LIMIT * 1024 * 1024
        ),
    )(*args)
    return pl.pallas_call(
        second_kernel,
        out_shape=tuple(jax.ShapeDtypeStruct((levels, rows, width), f32) for _ in range(4)),
        in_specs=[held] * 7,
        out_specs=(far,) * 4,
        scratch_shapes=[
            pltpu.VMEM((4 * levels, rows, width), f32),
            dma((nb, 4)),
        ],
        compiler_params=pltpu.CompilerParams(vmem_limit_bytes=LIMIT * 1024 * 1024),
    )(*middle)


def solution(mesh):
    grid, line = P(None, "lat", "lon"), P("lat", "lon")
    body = functools.partial(shards, mesh.shape["lat"], mesh.shape["lon"])
    return jax.shard_map(
        body, mesh=mesh, in_specs=(grid,) * 6 + (line,) * 3, out_specs=(grid,) * 4, check_vma=False
    )
```

```python
import functools

import jax
import jax.numpy as jnp
from jax import lax
from jax.experimental import pallas as pl
from jax.experimental.pallas import tpu as pltpu
from jax.sharding import PartitionSpec as P

time_step = 0.2
biharm_coef = 0.02
alpha_temp = 0.2
beta_salt = 0.8
thin_floor = 0.25

LANES = 128
LIMIT = 32
PAD = 8


def inverse(x):
    return pl.reciprocal(x, approx=True)


def loop(count, body):
    lax.fori_loop(0, count, lambda i, carry: (body(i), carry)[1], 0)


def edge_lanes():
    lane = lax.broadcasted_iota(jnp.int32, (8, LANES), 1)
    first, last = lane == 0, lane == LANES - 1

    def to_e(x, beside):
        return pltpu.roll(jnp.where(first, beside, x), LANES - 1, 1)

    def to_w(x, beside):
        return pltpu.roll(jnp.where(last, beside, x), 1, 1)

    return lane, to_e, to_w


def first_kernel(
    n_lat, n_lon,
    temp, salt, uvel, vvel, thick, land, east_width, north_width, coriolis,
    q, la, cor, lap, cf, pres, base,
    th, edge, row_pack, row_recv, col_pack, corner_pack, col_recv,
    whole_sem, edge_sem, in_sem, row_send, row_sem, col_send, col_sem, corner_send,
):
    levels, rows, width = temp.shape
    nc = width // LANES
    nb = rows // 8
    nf = 5 * levels + 2
    fa, fb = 5 * levels, 5 * levels + 1
    lat, lon = lax.axis_index("lat"), lax.axis_index("lon")
    top = lat == n_lat - 1
    south = lat > 0
    east_lon = lax.rem(lon + 1, n_lon)
    west_lon = lax.rem(lon + n_lon - 1, n_lon)
    lat_n = jnp.where(top, lat, lat + 1)
    lat_s = jnp.where(south, lat - 1, 0)
    north = (lat_n, jnp.where(top, n_lon - 1 - lon, lon))
    fold_e = lax.rem(2 * n_lon - 2 - lon, n_lon)
    fold_w = lax.rem(n_lon - lon, n_lon)
    north_e = (lat_n, jnp.where(top, fold_e, east_lon))
    north_w = (lat_n, jnp.where(top, fold_w, west_lon))
    e_self = jnp.logical_and(top, fold_e == lon)
    w_self = jnp.logical_and(top, fold_w == lon)
    e_far, w_far = jnp.logical_not(e_self), jnp.logical_not(w_self)
    east, west = (lat, east_lon), (lat, west_lon)

    barrier = pltpu.get_barrier_semaphore()

    def greet(where):
        pl.semaphore_signal(barrier, inc=1, device_id={"lat": where[0], "lon": where[1]}, device_id_type=pl.DeviceIdType.MESH)

    greet(east)
    greet(west)
    greet(north)

    @pl.when(e_far)
    def _():
        greet(north_e)

    @pl.when(w_far)
    def _():
        greet(north_w)

    @pl.when(south)
    def _():
        greet((lat_s, lon))
        greet((lat_s, east_lon))
        greet((lat_s, west_lon))

    def begin(src, dst, sem):
        copy = pltpu.make_async_copy(src, dst, sem)
        copy.start()
        return copy

    whole = [begin(land, la, whole_sem.at[0]), begin(thick, th, whole_sem.at[1])]
    loads = {}

    def begin_tile(c):
        cols = pl.ds(c * LANES, LANES)
        here = []
        for i, src in enumerate((temp, salt, uvel, vvel)):
            here.append(begin(
                src.at[:, :, cols], q.at[i * levels:(i + 1) * levels, c, PAD:PAD + rows],
                in_sem.at[c, i],
            ))
        for i, src in enumerate((east_width, north_width)):
            here.append(begin(src.at[:, cols], q.at[fa + i, c, PAD:PAD + rows], in_sem.at[c, 4 + i]))
        loads[c] = here

    begin_tile(0)
    begin_tile(nc - 1)
    edge_loads = []
    for side, lo in ((0, 0), (1, rows - 8)):
        for i, src in enumerate((temp, salt, uvel, vvel)):
            edge_loads.append(begin(
                src.at[:, lo:lo + 8], edge.at[side, i * levels:(i + 1) * levels], edge_sem.at[side, i]
            ))
        for i, src in enumerate((east_width, north_width)):
            edge_loads.append(begin(src.at[lo:lo + 8], edge.at[side, fa + i], edge_sem.at[side, 4 + i]))
    for c in range(1, nc - 1):
        begin_tile(c)
    late = begin(coriolis, cor, whole_sem.at[2])

    lane, to_e, to_w = edge_lanes()
    sub = lax.broadcasted_iota(jnp.int32, (8, LANES), 0)

    def finish_load(c):
        for copy in loads[c]:
            copy.wait()
        for l in range(levels):
            cols = slice(c * LANES, (c + 1) * LANES)
            q[4 * levels + l, c, PAD:PAD + rows, :] = la[l, :, cols].astype(jnp.float32) * th[l, :, cols]

    for copy in whole:
        copy.wait()

    finish_load(0)
    finish_load(nc - 1)
    own = [jnp.logical_and(lane >= 4 * f, lane < 4 * f + 4) for f in range(nf)]

    def pack_cols(k):
        r = pl.ds(pl.multiple_of(PAD + 8 * k, 8), 8)
        block = jnp.zeros((8, LANES), jnp.float32)
        for f in range(nf):
            ends = jnp.where(lane < LANES // 2, q[f, 0, r, :], q[f, nc - 1, r, :])
            block = jnp.where(own[f], pltpu.roll(ends, 4 * f + 2, 1), block)
        col_pack[k] = block

    loop(nb, pack_cols)
    sign_lane = jnp.where(
        jnp.logical_and(lane >= 8 * levels, lane < 16 * levels), -1.0, 1.0
    ).astype(jnp.float32)
    x = col_pack[nb - 1]
    place = lane % 4
    y = jnp.where(
        place < 2,
        jnp.where(place == 0, pltpu.roll(x, LANES - 3, 1), pltpu.roll(x, LANES - 1, 1)),
        jnp.where(place == 2, pltpu.roll(x, 1, 1), pltpu.roll(x, 3, 1)),
    ) * sign_lane
    y = jnp.where(sub == 0, pltpu.roll(y, 2, 0), pltpu.roll(y, 4, 0))
    corner_pack[...] = jnp.where(top, y, x)

    partners = 3 + e_far.astype(jnp.int32) + w_far.astype(jnp.int32) + 3 * south.astype(jnp.int32)
    pl.semaphore_wait(barrier, partners)

    def send(src, dst, s_sem, r_sem, where):
        return pltpu.make_async_remote_copy(
            src_ref=src, dst_ref=dst, send_sem=s_sem, recv_sem=r_sem,
            device_id={"lat": where[0], "lon": where[1]}, device_id_type=pl.DeviceIdType.MESH,
        )

    to_east = send(col_pack, col_recv.at[1, 1:nb + 1], col_send.at[1], col_sem.at[1, 1], east)
    to_west = send(col_pack, col_recv.at[0, 1:nb + 1], col_send.at[0], col_sem.at[0, 1], west)
    e_side = jnp.where(top, 0, 1)
    w_side = jnp.where(top, 1, 0)
    blk = jnp.where(top, nb + 1, 0)
    which = jnp.where(top, 2, 0)
    to_ne = send(corner_pack, col_recv.at[e_side, blk], corner_send.at[0], col_sem.at[e_side, which], north_e)
    to_nw = send(corner_pack, col_recv.at[w_side, blk], corner_send.at[1], col_sem.at[w_side, which], north_w)
    to_se = send(col_pack.at[0], col_recv.at[1, nb + 1], corner_send.at[2], col_sem.at[1, 2], (lat_s, east_lon))
    to_sw = send(col_pack.at[0], col_recv.at[0, nb + 1], corner_send.at[3], col_sem.at[0, 2], (lat_s, west_lon))
    to_east.start()
    to_west.start()

    @pl.when(south)
    def _():
        to_se.start()
        to_sw.start()

    @pl.when(e_far)
    def _():
        to_ne.start()

    @pl.when(w_far)
    def _():
        to_nw.start()

    for copy in edge_loads:
        copy.wait()
    flip = jnp.where(top, -1.0, 1.0).astype(jnp.float32)
    for side in range(2):
        for l in range(levels):
            f = 4 * levels + l
            lo = (rows - 8) * side
            edge[side, f] = la[l, lo:lo + 8].astype(jnp.float32) * th[l, lo:lo + 8]
    slot = jnp.where(top, 1, 0)
    to_north = send(row_pack.at[1], row_recv.at[slot], row_send.at[1], row_sem.at[slot], north)
    to_south = send(row_pack.at[0], row_recv.at[1], row_send.at[0], row_sem.at[1], (lat_s, lon))
    for f in range(nf):
        for c in range(nc):
            cols = slice(c * LANES, (c + 1) * LANES)
            row_pack[0, c, 2 * f:2 * f + 2, :] = edge[0, f, 0:2, cols]

    @pl.when(south)
    def _():
        to_south.start()

    for f in range(nf):
        for c in range(nc):
            cols = slice(c * LANES, (c + 1) * LANES)
            near = edge[1, f, 6:7, cols]
            far = jnp.where(top, edge[1, f, 5:6, cols], edge[1, f, 7:8, cols])
            if 2 * levels <= f < 4 * levels:
                near, far = near * flip, far * flip
            row_pack[1, c, 2 * f:2 * f + 1, :] = near
            row_pack[1, c, 2 * f + 1:2 * f + 2, :] = far

    @pl.when(top)
    def _():
        i0 = lax.broadcasted_iota(jnp.int32, (LANES, LANES), 0)
        i1 = lax.broadcasted_iota(jnp.int32, (LANES, LANES), 1)
        mirror = (i0 + i1 == LANES - 1).astype(jnp.float32)
        turned = [
            jnp.dot(row_pack[1, c, 0:2 * nf, :], mirror, precision=lax.Precision.HIGHEST,
                    preferred_element_type=jnp.float32)
            for c in range(nc)
        ]
        for c in range(nc):
            row_pack[1, nc - 1 - c, 0:2 * nf, :] = turned[c]

    to_north.start()

    for c in range(1, nc - 1):
        finish_load(c)
    ring = nc + 1

    def pass_a(s, c):
        cp, cm = (c + 1) % ring, (c - 1) % ring
        r0, rn, rs = pl.ds(s, 8), pl.ds(s + 1, 8), pl.ds(s - 1, 8)

        def five(f):
            x = q[f, c, r0, :]
            return (x, to_e(x, q[f, cp, r0, :]), to_w(x, q[f, cm, r0, :]), q[f, c, rn, :], q[f, c, rs, :])

        a, ae, aw, an, as_ = five(fa)
        b, be, bw, bn, bs = five(fb)
        area = a * b
        root = biharm_coef ** 0.5
        we, ww, wn, ws = b + be, b + bw, a + an, a + as_
        re, rw = (root * we) * inverse(a + ae), (root * ww) * inverse(a + aw)
        rn_, rs_ = (root * wn) * inverse(b + bn), (root * ws) * inverse(b + bs)
        k = time_step / 8.0
        we, ww, wn, ws = we * k, ww * k, wn * k, ws * k
        over = jnp.zeros_like(a)
        for l in range(levels):
            d, de, dw, dn, ds_ = five(4 * levels + l)
            inv = inverse(area * jnp.maximum(d, thin_floor))
            me = jnp.minimum(d, de) * inv
            mw = jnp.minimum(d, dw) * inv
            mn = jnp.minimum(d, dn) * inv
            ms = jnp.minimum(d, ds_) * inv
            ce, cw, cn, cs = me * re, mw * rw, mn * rn_, ms * rs_
            if c < nc:
                cf[l, c, r0, :] = ce
                cf[levels + l, c, r0, :] = cw
                cf[2 * levels + l, c, r0, :] = cn
                cf[3 * levels + l, c, r0, :] = cs

            def laplace(v, x, xe, xw, xn, xs):
                lap[v * levels + l, c, r0, :] = (
                    ce * (xe - x) + cw * (xw - x) + cn * (xn - x) + cs * (xs - x)
                )

            u = five(2 * levels + l)
            laplace(2, *u)
            te = me * we * (u[0] + u[1])
            tw = mw * ww * (u[0] + u[2])
            v = five(3 * levels + l)
            laplace(3, *v)
            tn = mn * wn * (v[0] + v[3])
            ts = ms * ws * (v[0] + v[4])
            tracer = []
            for i in range(2):
                x, xe, xw, xn, xs = five(i * levels + l)
                laplace(i, x, xe, xw, xn, xs)
                if c < nc:
                    advect = te * (x + xe) - tw * (x + xw) + tn * (x + xn) - ts * (x + xs)
                    base[i * levels + l, c, r0, :] = x - advect
                tracer.append(x)
            buoyancy = (beta_salt * tracer[1] - alpha_temp * tracer[0]) * d
            pres[l, c, r0, :] = over + 0.5 * buoyancy
            over = over + buoyancy

    def row_a(s, tiles):
        for c in tiles:
            pass_a(s, c)

    def unpack_cols(block):
        s = pl.multiple_of(8 * block, 8)
        both = jnp.where(lane % 4 < 2, col_recv[1, block], col_recv[0, block])
        for f in range(nf):
            q[f, nc, pl.ds(s, 8), :] = pltpu.roll(both, LANES - 2 - 4 * f, 1)

    loop(nb - 1, lambda k: row_a(PAD - 1 + 8 * (1 + k), range(1, nc - 1)))
    to_east.wait_recv()
    to_west.wait_recv()
    loop(nb, lambda i: unpack_cols(i + 1))
    loop(nb - 1, lambda k: row_a(PAD - 1 + 8 * (1 + k), (nc - 1, nc, 0)))

    @pl.when(south)
    def _():
        send(row_pack.at[1], row_recv.at[0], row_send.at[1], row_sem.at[0], north).wait_recv()
        send(corner_pack, col_recv.at[1, 0], corner_send.at[0], col_sem.at[1, 0], east).wait_recv()
        send(corner_pack, col_recv.at[0, 0], corner_send.at[1], col_sem.at[0, 0], west).wait_recv()
        for f in range(nf):
            q[f, 0:nc, PAD - 2:PAD, :] = row_recv[0, :, 2 * f:2 * f + 2, :]
        unpack_cols(0)

    @pl.when(jnp.logical_not(south))
    def _():
        for f in range(nf):
            q[f, :, 0:PAD, :] = jnp.full((ring, PAD, LANES), 1.0 if f >= fa else 0.0, jnp.float32)

    send(row_pack.at[0], row_recv.at[1], row_send.at[0], row_sem.at[1], north).wait_recv()

    @pl.when(e_far)
    def _():
        send(corner_pack, col_recv.at[0, nb + 1], corner_send.at[0], col_sem.at[0, 2], east).wait_recv()

    @pl.when(e_self)
    def _():
        col_recv[0, nb + 1] = corner_pack[...]

    @pl.when(w_far)
    def _():
        send(corner_pack, col_recv.at[1, nb + 1], corner_send.at[1], col_sem.at[1, 2], west).wait_recv()

    @pl.when(w_self)
    def _():
        col_recv[1, nb + 1] = corner_pack[...]

    for f in range(nf):
        q[f, 0:nc, PAD + rows:PAD + rows + 2, :] = row_recv[1, :, 2 * f:2 * f + 2, :]
    unpack_cols(nb + 1)

    loop(2, lambda i: row_a(PAD - 1 + (rows - 6) * i, range(ring)))

    late.wait()
    to_east.wait_send()
    to_west.wait_send()
    to_north.wait_send()

    @pl.when(south)
    def _():
        to_south.wait_send()
        to_se.wait_send()
        to_sw.wait_send()

    @pl.when(e_far)
    def _():
        to_ne.wait_send()

    @pl.when(w_far)
    def _():
        to_nw.wait_send()


def second_kernel(
    q, la, cor, lap, cf, pres, base, temp_out, salt_out, uvel_out, vvel_out,
    ob, out_sem,
):
    levels, rows, width = temp_out.shape
    nc, nb = width // LANES, rows // 8
    fa, fb = 5 * levels, 5 * levels + 1
    ring = nc + 1
    lane, to_e, to_w = edge_lanes()

    def pass_b(j, c):
        cp, cm = (c + 1) % ring, (c - 1) % ring
        s = pl.multiple_of(PAD + 8 * j, 8)
        t = pl.multiple_of(8 * j, 8)
        r0, rn, rs, ro = pl.ds(s, 8), pl.ds(s + 1, 8), pl.ds(s - 1, 8), pl.ds(t, 8)
        cols = slice(c * LANES, (c + 1) * LANES)
        ga = (0.5 * time_step) * inverse(q[fa, c, r0, :])
        gb = (0.5 * time_step) * inverse(q[fb, c, r0, :])
        rot = time_step * cor[ro, cols]
        for l in range(levels):
            ce, cw = cf[l, c, r0, :], cf[levels + l, c, r0, :]
            cn, cs = cf[2 * levels + l, c, r0, :], cf[3 * levels + l, c, r0, :]
            wet = la[l, ro, cols].astype(jnp.float32)

            def drag(v):
                f = v * levels + l
                x = lap[f, c, r0, :]
                xe, xw = to_e(x, lap[f, cp, r0, :]), to_w(x, lap[f, cm, r0, :])
                xn, xs = lap[f, c, rn, :], lap[f, c, rs, :]
                return ce * (xe - x) + cw * (xw - x) + cn * (xn - x) + cs * (xs - x)

            for i in range(2):
                ob[i * levels + l, ro, cols] = wet * (base[i * levels + l, c, r0, :] - drag(i))
            p = pres[l, c, r0, :]
            ge = (to_e(p, pres[l, cp, r0, :]) - to_w(p, pres[l, cm, r0, :])) * ga
            gn = (pres[l, c, rn, :] - pres[l, c, rs, :]) * gb
            u, v = q[2 * levels + l, c, r0, :], q[3 * levels + l, c, r0, :]
            ob[2 * levels + l, ro, cols] = wet * (u + (rot * v - ge) - drag(2))
            ob[3 * levels + l, ro, cols] = wet * (v - (rot * u + gn) - drag(3))

    outs = (temp_out, salt_out, uvel_out, vvel_out)

    def store(j):
        t = pl.multiple_of(8 * j, 8)
        return [
            pltpu.make_async_copy(
                ob.at[i * levels:(i + 1) * levels, pl.ds(t, 8)], dst.at[:, pl.ds(t, 8)], out_sem.at[j, i]
            )
            for i, dst in enumerate(outs)
        ]

    def row_b(j):
        for c in range(nc):
            pass_b(j, c)
        for copy in store(j):
            copy.start()

    def settle(j):
        for copy in store(j):
            copy.wait()

    loop(nb, row_b)
    loop(nb, settle)


def shards(n_lat, n_lon, *args):
    levels, rows, width = args[0].shape
    nc, nb, nf = width // LANES, rows // 8, 5 * levels + 2
    tall = rows + 2 * PAD
    row_slots = -(-2 * nf // 8) * 8
    f32 = jnp.float32

    def plane(count):
        return pltpu.VMEM((count, nc + 1, tall, LANES), f32)

    dma = pltpu.SemaphoreType.DMA
    held = pl.BlockSpec(memory_space=pltpu.VMEM)
    far = pl.BlockSpec(memory_space=pl.ANY)
    args = [pltpu.with_memory_space_constraint(x, pltpu.HBM) for x in args]
    middle = pl.pallas_call(
        functools.partial(first_kernel, n_lat, n_lon),
        out_shape=(
            plane(nf),
            pltpu.VMEM((levels, rows, width), jnp.int32),
            pltpu.VMEM((rows, width), f32),
            plane(4 * levels),
            plane(4 * levels),
            plane(levels),
            plane(2 * levels),
        ),
        in_specs=[far] * 9,
        out_specs=(held,) * 7,
        scratch_shapes=[
            pltpu.VMEM((levels, rows, width), f32),
            pltpu.VMEM((2, nf, 8, width), f32),
            pltpu.VMEM((2, nc, row_slots, LANES), f32),
            pltpu.VMEM((2, nc, row_slots, LANES), f32),
            pltpu.VMEM((nb, 8, LANES), f32),
            pltpu.VMEM((8, LANES), f32),
            pltpu.VMEM((2, nb + 2, 8, LANES), f32),
            dma((3,)),
            dma((2, 6)),
            dma((nc, 6)),
            dma((2,)),
            dma((2,)),
            dma((2,)),
            dma((2, 3)),
            dma((4,)),
        ],
        compiler_params=pltpu.CompilerParams(
            collective_id=0, has_side_effects=True, vmem_limit_bytes=LIMIT * 1024 * 1024
        ),
    )(*args)
    return pl.pallas_call(
        second_kernel,
        out_shape=tuple(jax.ShapeDtypeStruct((levels, rows, width), f32) for _ in range(4)),
        in_specs=[held] * 7,
        out_specs=(far,) * 4,
        scratch_shapes=[
            pltpu.VMEM((4 * levels, rows, width), f32),
            dma((nb, 4)),
        ],
        compiler_params=pltpu.CompilerParams(vmem_limit_bytes=LIMIT * 1024 * 1024),
    )(*middle)


def solution(mesh):
    grid, line = P(None, "lat", "lon"), P("lat", "lon")
    body = functools.partial(shards, mesh.shape["lat"], mesh.shape["lon"])
    return jax.shard_map(
        body, mesh=mesh, in_specs=(grid,) * 6 + (line,) * 3, out_specs=(grid,) * 4, check_vma=False
    )
```
